32 devices in a mesh: row: 4 (over z), col: 4 (over y, x), rep: 2 (over core).
Axes of the slice: x: 2, y: 2, z: 4, core: 2. Of those that a mesh axis runs over, the one named last changes fastest.
Arguments:
- amplitudes: bfloat16 [4096, 8192], P('row', ('rep', 'col')), may hold values from -6 to 6
- integrals: bfloat16 [8192, 4096], P(('rep', 'row'), 'col'), may hold values from -0.09375 to 0.09375
- tile_mask: int32 [64, 32], replicated, may hold values from 0 to 1
- k_irrep: int32 [64], replicated, may hold values from 0 to 3
- n_irrep: int32 [32], replicated, may hold values from 0 to 3
- stored_tile: int32 [64], replicated, may hold values from 0 to 63, as said below
Outputs:
- ladder: bfloat16 [4096, 4096], P('row', ('col', 'rep'))
The draws below stay inside these ranges and needn't reach their ends.
Inputs may be any that keep to these rules, and one draw needn't show every extreme that they name: `stored_tile`: for each q, slots q * 32 to (q + 1) * 32 - 1 hold a permutation of the tiles q * 32 to (q + 1) * 32 - 1.
All inputs are finite; a program needn't handle non-finite values.
Results may differ from the reference program's by a relative error of at most 0.001.
Values may be sent and summed in bfloat16 or wider, within the bound.
A program may use at most 128 MiB of HBM per device.

```python
import jax
import jax.numpy as jnp

TS = 128
NCOL = 1024
M = 4096
K = 8192
N = 4096
KS = 32
KT = 64
NT = 32


def draw_stored_tile(key, part):
    scores = jax.random.randint(key, (KT,), 0, 1 << 20) * KT + jnp.arange(KT, dtype=jnp.int32)
    grouped = scores.reshape(KT // KS, KS)
    order = jnp.argsort(grouped, axis=1, stable=True).astype(jnp.int32)
    offsets = (jnp.arange(KT // KS, dtype=jnp.int32) * KS)[:, None]
    return (order + offsets).reshape(KT).astype(jnp.int32)


def dense_choice(key):
    seed_key = jax.random.fold_in(key, 7001)
    dense_slab = jax.random.randint(jax.random.fold_in(seed_key, 1), (), 0, KT // KS).astype(jnp.int32)
    dense_col = jax.random.randint(jax.random.fold_in(seed_key, 2), (), 0, NT // (NCOL // TS)).astype(jnp.int32)
    dense_label = jax.random.randint(jax.random.fold_in(seed_key, 3), (), 0, 4).astype(jnp.int32)
    return (dense_slab, dense_col, dense_label)


def slab_ids():
    return (jnp.arange(KT, dtype=jnp.int32) // KS).astype(jnp.int32)


def column_ids():
    return (jnp.arange(NT, dtype=jnp.int32) // (NCOL // TS)).astype(jnp.int32)


def draw_k_irrep(key, part):
    dense_slab, dense_col, dense_label = dense_choice(key)
    base_labels = jax.random.randint(jax.random.fold_in(key, 7101), (KT,), 0, 4).astype(jnp.int32)
    return jnp.where(slab_ids() == dense_slab, dense_label, base_labels).astype(jnp.int32)


def draw_n_irrep(key, part):
    dense_slab, dense_col, dense_label = dense_choice(key)
    base_labels = jax.random.randint(jax.random.fold_in(key, 7201), (NT,), 0, 4).astype(jnp.int32)
    return jnp.where(column_ids() == dense_col, dense_label, base_labels).astype(jnp.int32)


def draw_tile_mask(key, part):
    dense_slab, dense_col, dense_label = dense_choice(key)
    base_draw = jax.random.randint(jax.random.fold_in(key, 7301), (KT, NT), 0, 4)
    base_mask = (base_draw < 3).astype(jnp.int32)
    inside = jnp.logical_and((slab_ids() == dense_slab)[:, None], (column_ids() == dense_col)[None, :])
    return jnp.where(inside, 1, base_mask).astype(jnp.int32)


def strengthened(array, rng, source, target, blocks, factor):
    owner, partner = [(jnp.arange(array.shape[dim]) // (array.shape[dim] // blocks)).reshape([-1 if axis == dim else 1 for axis in range(array.ndim)]) for dim in (source, target)]
    chosen = jax.random.permutation(rng, blocks)[partner]
    strong = (owner == chosen) | (owner == (partner + blocks // 2) % blocks)
    return jnp.where(strong, factor * array, array)


def shard_levels(key, dims, shards, smallest, largest):
    def one(axis_at, parts):
        draws = jax.random.uniform(jax.random.fold_in(jax.random.fold_in(key, 6), axis_at), (parts,), jnp.float32, smallest / len(shards), largest / len(shards))
        return jnp.repeat(jnp.exp(draws), dims[axis_at] // parts).reshape((-1,) + (1,) * (len(dims) - axis_at - 1))

    level = one(*shards[0])
    for cut in shards[1:]:
        level = level * one(*cut)
    return level


def normal_values(rng, shape, deviation, bound, pieces=(), kind=jnp.bfloat16):
    values = jax.random.normal(rng, shape, jnp.float32) * deviation
    if len(pieces) > 0:
        values = shard_levels(rng, shape, pieces, -0.22, 0.18) * values
    return jnp.clip(values, min=-bound, max=bound).astype(kind)


def heavy_noise(own_key, shape, width, limit, pieces, heavy, kind=jnp.bfloat16):
    entries = width * jax.random.normal(own_key, shape, jnp.float32)
    if pieces:
        entries = entries * shard_levels(own_key, shape, pieces, -0.22, 0.18)
    return jnp.clip(strengthened(entries, jax.random.fold_in(own_key, 3), *heavy), -limit, limit).astype(kind)


def setup_inputs(seed: int = 0) -> dict:
    seeds = jax.random.split(jax.random.key(seed), 7)
    amplitudes = normal_values(seeds[0], (M, K), 1.0, 6.0, ((0, 4), (1, 8)))
    integrals = heavy_noise(seeds[1], (K, N), K ** -0.5, 0.09375, ((0, 8), (1, 4)), (0, 1, 8, 2.0))
    tile_mask = draw_tile_mask(jax.random.fold_in(seeds[6], 71), 0)
    k_irrep = draw_k_irrep(jax.random.fold_in(seeds[6], 71), 0)
    n_irrep = draw_n_irrep(jax.random.fold_in(seeds[6], 71), 0)
    stored_tile = draw_stored_tile(jax.random.fold_in(seeds[6], 71), 0)
    return {"amplitudes": amplitudes, "integrals": integrals, "tile_mask": tile_mask, "k_irrep": k_irrep, "n_irrep": n_irrep, "stored_tile": stored_tile}


def reference(amplitudes, integrals, tile_mask, k_irrep, n_irrep, stored_tile):
    allowed = jnp.logical_and(k_irrep[:, None] == n_irrep[None, :], tile_mask == 1)
    allowed_slots = jnp.take(allowed, stored_tile, axis=0).astype(jnp.bfloat16)
    blocks = integrals.reshape(KT, TS, NT, TS) * allowed_slots[:, None, :, None]
    ordered = jnp.take(amplitudes.reshape(M, KT, TS), stored_tile, axis=1).reshape(M, K)
    return jnp.dot(ordered, blocks.reshape(K, N), preferred_element_type=jnp.float32).astype(jnp.bfloat16)
```

```python
import functools

import jax
import jax.numpy as jnp
from jax import lax
from jax.experimental import pallas as pl
from jax.experimental.pallas import tpu as pltpu
from jax.sharding import PartitionSpec as P

TS = 128
PARTS = 4


def remote(src, dst, send_sem, recv_sem, **target):
    return pltpu.make_async_remote_copy(
        src_ref=src,
        dst_ref=dst,
        send_sem=send_sem,
        recv_sem=recv_sem,
        device_id=target,
        device_id_type=pl.DeviceIdType.MESH,
    )


def kernel(
    rows_n,
    a_ref,
    b_ref,
    mask_ref,
    k_ref,
    n_ref,
    stored_ref,
    out_ref,
    a_all,
    a_ord,
    b_all,
    part_out,
    part_in,
    own_sem,
    a_send,
    a_recv,
    b_up,
    b_down,
    b_recv,
    p_send,
    p_recv,
):
    z = lax.axis_index("row")
    c = lax.axis_index("col")
    r = lax.axis_index("rep")
    last = rows_n - 1
    x = lax.rem(c, 2)
    y = lax.div(c, 2)
    xn = y * 2 + (1 - x)
    yn = (1 - y) * 2 + x
    diag = (1 - y) * 2 + (1 - x)
    mrow, kcol = a_ref.shape
    kb, ncol = b_ref.shape
    slots = kb // TS
    slab_tiles = slots * rows_n
    ra = mrow // PARTS
    cb = ncol // PARTS

    per = kcol // TS
    own = [
        pltpu.make_async_copy(a_ref.at[:, pl.ds(t * TS, TS)], a_all.at[c * per + t], own_sem.at[t])
        for t in range(per)
    ]
    for copy in own:
        copy.start()

    barrier = pltpu.get_barrier_semaphore()
    mesh_id = pl.DeviceIdType.MESH
    pl.semaphore_signal(barrier, inc=1, device_id={"col": xn}, device_id_type=mesh_id)
    pl.semaphore_signal(barrier, inc=1, device_id={"col": yn}, device_id_type=mesh_id)
    pl.semaphore_signal(barrier, inc=1, device_id={"rep": 1 - r}, device_id_type=mesh_id)

    @pl.when(z > 0)
    def _():
        pl.semaphore_signal(barrier, inc=1, device_id={"row": z - 1}, device_id_type=mesh_id)

    @pl.when(z < last)
    def _():
        pl.semaphore_signal(barrier, inc=1, device_id={"row": z + 1}, device_id_type=mesh_id)

    pl.semaphore_wait(barrier, 3 + jnp.where(z > 0, 1, 0) + jnp.where(z < last, 1, 0))

    for copy in own:
        copy.wait()

    def block(owner, i):
        return a_all.at[pl.ds(owner * per, per), pl.ds(i * ra, ra), :]

    def to_x(owner, i, k, kind):
        view = block(owner, i)
        return remote(view, view, a_send.at[0, k], a_recv.at[kind, i], col=xn)

    def to_y(owner, i, k, kind):
        view = block(owner, i)
        return remote(view, view, a_send.at[1, k], a_recv.at[kind, i], col=yn)

    sends = []
    for i in range(PARTS):
        sends.append(to_x(c, i, i, 0))
        sends[-1].start()
        k = (i + PARTS // 2) % PARTS
        sends.append(to_y(c, k, k, 1))
        sends[-1].start()

    def a_got(kind, i):
        owner = (xn, yn, diag)[kind]
        view = block(owner, i)
        return remote(view, view, a_send.at[0, 0], a_recv.at[kind, i], col=xn)

    def bcols(j):
        q = lax.rem(j + (PARTS // 2) * (1 - r), PARTS)
        return pl.ds(pl.multiple_of(q * cb, cb), cb), q

    def b_copy(s, j, up):
        cols, _ = bcols(j)
        sems = b_up if up else b_down
        view = b_all.at[s, :, cols]
        return remote(view, view, sems.at[s, j], b_recv.at[s, j], row=z + 1 if up else z - 1)

    def pass_up(s, j):
        @pl.when(z < last)
        def _():
            b_copy(s, j, True).start()

    def pass_down(s, j):
        @pl.when(z > 0)
        def _():
            b_copy(s, j, False).start()

    for j in range(PARTS):
        _, q = bcols(j)

        def mask_slot(t, carry, q=q):
            k = stored_ref[r * slab_tiles + z * slots + t]
            rows = pl.ds(pl.multiple_of(t * TS, TS), TS)
            for n in range(cb // TS):
                nt = q * (cb // TS) + n
                g = c * (ncol // TS) + nt
                ok = jnp.logical_and(k_ref[k] == n_ref[g], mask_ref[k, g] == 1)
                cols = pl.ds(pl.multiple_of(nt * TS, TS), TS)
                weight = jnp.where(ok, 1.0, 0.0).astype(jnp.float32)
                b_all[z, rows, cols] = (b_ref[rows, cols].astype(jnp.float32) * weight).astype(
                    jnp.bfloat16
                )
            return carry

        lax.fori_loop(0, slots, mask_slot, 0)
        pass_up(z, j)
        pass_down(z, j)

    for j in range(PARTS):
        if j < PARTS // 2:
            a_got(0, j).wait_recv()
            relay = to_y(xn, j, PARTS + j, 2)
            relay.start()
            sends.append(relay)
            k = j + PARTS // 2
            a_got(1, k).wait_recv()
            relay = to_x(yn, k, PARTS + j, 2)
            relay.start()
            sends.append(relay)

        @pl.when(jnp.logical_and(z > 0, z < last))
        def _(j=j):
            b_copy(z - 1, j, True).wait_recv()
            pass_up(z - 1, j)
            b_copy(z + 1, j, False).wait_recv()
            pass_down(z + 1, j)

    for d in range(2, rows_n - 1):
        for j in range(PARTS):

            @pl.when(jnp.logical_and(z - d >= 0, z < last))
            def _(d=d, j=j):
                b_copy(z - d, j, True).wait_recv()
                pass_up(z - d, j)

            @pl.when(jnp.logical_and(z + d <= last, z > 0))
            def _(d=d, j=j):
                b_copy(z + d, j, False).wait_recv()
                pass_down(z + d, j)

    for i in range(PARTS // 2):
        a_got(0, i + PARTS // 2).wait_recv()
        a_got(1, i).wait_recv()
    for i in range(PARTS):
        a_got(2, i).wait_recv()

    def order(s, carry):
        t = jnp.maximum(stored_ref[r * slab_tiles + s] - r * slab_tiles, 0)
        lane = pl.multiple_of(lax.rem(s, slots) * TS, TS)
        a_ord[lax.div(s, slots), :, pl.ds(lane, TS)] = a_all[t]
        return carry

    lax.fori_loop(0, slab_tiles, order, 0)

    def rest(j):
        @pl.when(z == 0)
        def _():
            for s in range(1, rows_n):
                b_copy(s, j, False).wait_recv()

        @pl.when(z == last)
        def _():
            for s in range(last):
                b_copy(s, j, True).wait_recv()

    def product(j, i):
        cols, _ = bcols(j)
        rows = pl.ds(pl.multiple_of(i * ra, ra), ra)
        total = jnp.zeros((ra, cb), jnp.float32)
        for s in range(rows_n):
            total += jnp.dot(
                a_ord[s, rows, :], b_all[s, :, cols], preferred_element_type=jnp.float32
            )
        return rows, total

    swaps = []
    for j in range(PARTS // 2):
        rest(j)

        def away(i, carry, j=j):
            rows, total = product(j, i)
            part_out[j, rows, :] = total
            return carry

        lax.fori_loop(0, PARTS, away, 0)
        swap = remote(part_out.at[j], part_in.at[j], p_send.at[j], p_recv.at[j], rep=1 - r)
        swap.start()
        swaps.append(swap)

    for h in range(PARTS // 2):
        j = h + PARTS // 2
        rest(j)
        swaps[h].wait_recv()

        def stay(i, carry, j=j, h=h):
            rows, total = product(j, i)
            out_ref[rows, pl.ds(h * cb, cb)] = (total + part_in[h, rows, :]).astype(jnp.bfloat16)
            return carry

        lax.fori_loop(0, PARTS, stay, 0)

    for swap in swaps:
        swap.wait_send()
    for copy in sends:
        copy.wait_send()
    for j in range(PARTS):

        @pl.when(z < last)
        def _(j=j):
            b_copy(z, j, True).wait_send()

        @pl.when(z > 0)
        def _(j=j):
            b_copy(z, j, False).wait_send()

        for d in range(1, rows_n - 1):

            @pl.when(jnp.logical_and(z - d >= 0, z < last))
            def _(d=d, j=j):
                b_copy(z - d, j, True).wait_send()

            @pl.when(jnp.logical_and(z + d <= last, z > 0))
            def _(d=d, j=j):
                b_copy(z + d, j, False).wait_send()


def fused(rows_n, cols_n, amplitudes, integrals, tile_mask, k_irrep, n_irrep, stored_tile):
    mrow, kcol = amplitudes.shape
    kb, ncol = integrals.shape
    half = ncol // 2
    cb = ncol // PARTS
    smem = pl.BlockSpec(memory_space=pltpu.SMEM)
    vmem = pl.BlockSpec(memory_space=pltpu.VMEM)
    return pl.pallas_call(
        functools.partial(kernel, rows_n),
        out_shape=jax.ShapeDtypeStruct((mrow, half), jnp.bfloat16),
        in_specs=[pl.BlockSpec(memory_space=pl.ANY), vmem, smem, smem, smem, smem],
        out_specs=vmem,
        scratch_shapes=[
            pltpu.VMEM((cols_n * kcol // TS, mrow, TS), jnp.bfloat16),
            pltpu.VMEM((rows_n, mrow, kb), jnp.bfloat16),
            pltpu.VMEM((rows_n, kb, ncol), jnp.bfloat16),
            pltpu.VMEM((PARTS // 2, mrow, cb), jnp.float32),
            pltpu.VMEM((PARTS // 2, mrow, cb), jnp.float32),
            pltpu.SemaphoreType.DMA((kcol // TS,)),
            pltpu.SemaphoreType.DMA((2, PARTS + PARTS // 2)),
            pltpu.SemaphoreType.DMA((3, PARTS)),
            pltpu.SemaphoreType.DMA((rows_n, PARTS)),
            pltpu.SemaphoreType.DMA((rows_n, PARTS)),
            pltpu.SemaphoreType.DMA((rows_n, PARTS)),
            pltpu.SemaphoreType.DMA((PARTS // 2,)),
            pltpu.SemaphoreType.DMA((PARTS // 2,)),
        ],
        compiler_params=pltpu.CompilerParams(
            collective_id=0, has_side_effects=True, vmem_limit_bytes=48 << 20
        ),
        cost_estimate=pl.CostEstimate(
            flops=2 * mrow * kb * rows_n * ncol,
            bytes_accessed=2 * (mrow * kcol + kb * ncol + mrow * half),
            transcendentals=0,
        ),
    )(amplitudes, integrals, tile_mask, k_irrep, n_irrep, stored_tile)


def gathered_form(amplitudes, integrals, tile_mask, k_irrep, n_irrep, stored_tile):
    slab = lax.axis_index("rep")
    column = lax.axis_index("col")
    place = lax.axis_index("row")
    kb, ncol = integrals.shape
    tiles_col = ncol // TS
    own = kb // TS
    slab_tiles = own * lax.axis_size("row")
    n_labels = lax.dynamic_slice_in_dim(n_irrep, column * tiles_col, tiles_col)
    mask_cols = lax.dynamic_slice_in_dim(tile_mask, column * tiles_col, tiles_col, 1)
    slots = lax.dynamic_slice_in_dim(stored_tile, slab * slab_tiles, slab_tiles)
    mine = lax.dynamic_slice_in_dim(slots, place * own, own)
    same = jnp.take(k_irrep, mine)[:, None] == n_labels[None, :]
    weights = jnp.logical_and(same, jnp.take(mask_cols, mine, axis=0) == 1).astype(jnp.bfloat16)
    shaped = integrals.reshape(own, TS, tiles_col, TS) * weights[:, None, :, None]
    masked = lax.all_gather(shaped.reshape(kb, ncol), "row", axis=0, tiled=True)
    amp_slab = lax.all_gather(amplitudes, "col", axis=1, tiled=True)
    mrow, kq = amp_slab.shape
    ordered = jnp.take(
        amp_slab.reshape(mrow, slab_tiles, TS), slots - slab * slab_tiles, axis=1
    ).reshape(mrow, kq)
    partial_value = jnp.dot(ordered, masked, preferred_element_type=jnp.float32)
    return lax.psum_scatter(partial_value, "rep", scatter_dimension=1, tiled=True).astype(
        jnp.bfloat16
    )


def solution(mesh):
    rows_n, cols_n, reps = (mesh.shape[name] for name in ("row", "col", "rep"))
    if (rows_n, cols_n, reps) == (4, 4, 2):
        body = functools.partial(fused, rows_n, cols_n)
    else:
        body = gathered_form
    placed = (P("row", ("rep", "col")), P(("rep", "row"), "col"), P(), P(), P(), P())
    return jax.shard_map(
        body, mesh=mesh, in_specs=placed, out_specs=P("row", ("col", "rep")), check_vma=False
    )
```

```python
import functools

import jax
import jax.numpy as jnp
from jax import lax
from jax.experimental import pallas as pl
from jax.experimental.pallas import tpu as pltpu
from jax.sharding import PartitionSpec as P

TS = 128
PARTS = 4


def remote(src, dst, send_sem, recv_sem, **target):
    return pltpu.make_async_remote_copy(
        src_ref=src,
        dst_ref=dst,
        send_sem=send_sem,
        recv_sem=recv_sem,
        device_id=target,
        device_id_type=pl.DeviceIdType.MESH,
    )


def kernel(
    a_ref,
    b_ref,
    mask_ref,
    k_ref,
    n_ref,
    stored_ref,
    out_ref,
    a_0,
    a_1,
    a_2,
    a_3,
    a_ord,
    a_far,
    b_all,
    part_out,
    part_in,
    fp_out,
    f_in,
    f_out,
    own_sem,
    a_send,
    a_recv,
    b_send,
    b_recv,
    far_send,
    far_recv,
    fp_send,
    fp_recv,
    f_send,
    f_recv,
    p_send,
    p_recv,
):
    a_all = (a_0, a_1, a_2, a_3)
    z = lax.axis_index("row")
    c = lax.axis_index("col")
    r = lax.axis_index("rep")
    rows_n = b_all.shape[0]
    end = jnp.logical_or(z == 0, z == rows_n - 1)
    inner = jnp.logical_not(end)
    near = 2 * (z // 2)
    far = 2 - near
    buddy = z + 1 - 2 * (z % 2)
    across = rows_n - 1 - z
    beyond = rows_n - 1 - buddy
    x = c % 2
    y = c // 2
    xn = y * 2 + (1 - x)
    yn = (1 - y) * 2 + x
    diag = (1 - y) * 2 + (1 - x)
    mrow, kcol = a_ref.shape
    kb, ncol = b_ref.shape
    half = ncol // 2
    slots = kb // TS
    slab_tiles = slots * rows_n
    per = kcol // TS
    ra = mrow // PARTS
    steps = half // TS
    mesh_id = pl.DeviceIdType.MESH

    own = [
        pltpu.make_async_copy(
            a_ref.at[pl.ds(i * ra, ra), pl.ds(t * TS, TS)],
            a_all[i].at[c * per + t],
            own_sem.at[i, t],
        )
        for i in range(PARTS)
        for t in range(per)
    ]
    for copy in own:
        copy.start()

    barrier = pltpu.get_barrier_semaphore()
    pl.semaphore_signal(barrier, inc=1, device_id={"col": xn}, device_id_type=mesh_id)
    pl.semaphore_signal(barrier, inc=1, device_id={"col": yn}, device_id_type=mesh_id)
    pl.semaphore_signal(barrier, inc=1, device_id={"rep": 1 - r}, device_id_type=mesh_id)
    pl.semaphore_signal(barrier, inc=1, device_id={"row": buddy}, device_id_type=mesh_id)

    @pl.when(inner)
    def _():
        pl.semaphore_signal(barrier, inc=1, device_id={"row": across}, device_id_type=mesh_id)

    pl.semaphore_wait(barrier, 4 + jnp.where(inner, 1, 0))

    for copy in own:
        copy.wait()

    def rows(i):
        return pl.ds(i * ra, ra)

    def a_copy(kind, i, receive=False):
        link = kind % 2
        if kind < 2:
            owner = (xn, yn)[link] if receive else c
            view = a_all[i].at[pl.ds(owner * per, per)]
        else:
            owner = diag if receive else (yn, xn)[link]
            part = pl.ds(link * (ra // 2), ra // 2)
            view = a_all[i].at[pl.ds(owner * per, per), part, :]
        return remote(view, view, a_send.at[kind, i], a_recv.at[kind, i], col=(xn, yn)[link])

    def a_own(i):
        if i < PARTS:
            a_copy(0, i).start()
            a_copy(1, i).start()

    def a_pass(i):
        a_copy(0, i, True).wait_recv()
        a_copy(3, i).start()
        a_copy(1, i, True).wait_recv()
        a_copy(2, i).start()

    def a_done(i):
        a_copy(2, i, True).wait_recv()
        a_copy(3, i, True).wait_recv()

    def tile_of(j):
        p = j // 2
        return ((1 - r) if j % 2 == 0 else r) * steps + p

    def lanes(t):
        return pl.ds(pl.multiple_of(t * TS, TS), TS)

    def b_copy(kind, j, receive=False):
        if receive:
            owner = (buddy, across, beyond)[kind]
        else:
            owner = (z, z, buddy)[kind]
        view = b_all.at[owner, :, lanes(tile_of(j))]
        target = buddy if kind == 0 else across
        return remote(view, view, b_send.at[kind, j], b_recv.at[kind, j], row=target)

    def far_copy(kind, i, receive=False):
        side = x if i % 2 == 0 else y
        if kind == 0:
            src = a_far if receive else a_ord
            first = 0 if receive else far
            return remote(
                src.at[first + side, rows(i), :],
                a_far.at[side, rows(i), :],
                far_send.at[0, i],
                far_recv.at[0, i],
                row=buddy,
            )
        view = a_far.at[(1 - side) if receive else side, rows(i), :]
        return remote(
            view, view, far_send.at[1, i], far_recv.at[1, i], col=xn if i % 2 == 0 else yn
        )

    def fp_copy(i, p):
        return remote(
            fp_out.at[i, p], f_in.at[i, p], fp_send.at[i, p], fp_recv.at[i, p], rep=1 - r
        )

    def f_copy(i, p):
        return remote(
            f_out.at[i, p], f_in.at[i, p], f_send.at[i, p], f_recv.at[i, p], row=buddy
        )

    def swap():
        return remote(part_out, part_in, p_send.at[0], p_recv.at[0], rep=1 - r)

    def order(block, i):
        def one(s, carry):
            t = jnp.maximum(stored_ref[r * slab_tiles + block * slots + s] - r * slab_tiles, 0)
            a_ord[block, rows(i), lanes(s)] = a_all[i][t]
            return carry

        lax.fori_loop(0, slots, one, 0)

    def mask(j):
        tile = tile_of(j)
        g = c * (ncol // TS) + tile

        def one(t, carry):
            k = stored_ref[r * slab_tiles + z * slots + t]
            ok = jnp.logical_and(k_ref[k] == n_ref[g], mask_ref[k, g] == 1)
            weight = jnp.where(ok, 1.0, 0.0).astype(jnp.float32)
            at = pl.ds(pl.multiple_of(t * TS, TS), TS)
            value = b_ref[at, lanes(tile)].astype(jnp.float32) * weight
            b_all[z, at, lanes(tile)] = value.astype(jnp.bfloat16)
            return carry

        lax.fori_loop(0, slots, one, 0)

    def product(first, count, side):
        cols = pl.ds(pl.multiple_of(side * half, half), half)

        def one(i):
            at = pl.ds(pl.multiple_of(i * ra, ra), ra)
            total = jnp.zeros((ra, half), jnp.float32)
            for s in range(count):
                total += jnp.dot(
                    a_ord[first + s, at, :],
                    b_all[first + s, :, cols],
                    preferred_element_type=jnp.float32,
                )
            return at, total

        return one

    def send_partial(first, count):
        part = product(first, count, 1 - r)

        def away(i, carry):
            at, total = part(i)
            part_out[at, :] = total
            return carry

        lax.fori_loop(0, PARTS, away, 0)
        swap().start()

    def far_dot(i, j):
        total = jnp.zeros((ra, TS), jnp.float32)
        for s in range(2):
            total += jnp.dot(
                a_far[s, rows(i), :],
                b_all[far + s, :, lanes(tile_of(j))],
                preferred_element_type=jnp.float32,
            )
        return total

    def far_steps(pairs):
        for i, p in pairs:
            fp_out[i, p] = far_dot(i, 2 * p)
            fp_copy(i, p).start()
        for i, p in pairs:
            total = far_dot(i, 2 * p + 1)
            fp_copy(i, p).wait_recv()
            f_out[i, p] = total + f_in[i, p]
            f_copy(i, p).start()

    a_own(0)
    a_own(1)
    chunks = 2 * steps

    @pl.when(end)
    def _():
        for j in range(chunks):
            mask(j)
            if j < PARTS:
                b_copy(0, j).start()
        sent = PARTS
        for i in range(PARTS):
            a_pass(i)
            a_own(i + 2)
            a_done(i)
            side = x if i % 2 == 0 else y
            order(far + side, i)
            far_copy(0, i).start()
            more = (0, 2, 1, chunks)[i]
            for j in range(sent, min(chunks, sent + more)):
                b_copy(0, j).start()
            sent = min(chunks, sent + more)
        for i in range(PARTS):
            order(near, i)
            order(near + 1, i)
        for j in range(chunks):
            b_copy(0, j, True).wait_recv()
        send_partial(near, 2)
        part = product(near, 2, r)

        def stay(i, carry):
            at, total = part(i)
            for p in range(steps):
                f_out[i, p] = total[:, p * TS : (p + 1) * TS]
            return carry

        lax.fori_loop(0, PARTS, stay, 0)
        swap().wait_recv()
        for i, p in FAR_ORDER:
            f_copy(i, p).wait_recv()
            cols = pl.ds(p * TS, TS)
            value = f_out[i, p] + part_in[rows(i), cols] + f_in[i, p]
            out_ref[rows(i), cols] = value.astype(jnp.bfloat16)
        for i in range(PARTS):
            far_copy(0, i).wait_send()

    @pl.when(inner)
    def _():
        def pass_b(j):
            b_copy(1, j).start()
            b_copy(0, j, True).wait_recv()
            b_copy(2, j).start()

        def far_pass(i):
            far_copy(0, i, True).wait_recv()
            far_copy(1, i).start()

        def far_b(p):
            for j in (2 * p, 2 * p + 1):
                b_copy(1, j, True).wait_recv()
                b_copy(2, j, True).wait_recv()

        for j in range(chunks):
            mask(j)
            b_copy(0, j).start()
        pass_b(0)
        pass_b(1)
        a_pass(0)
        a_own(2)
        pass_b(2)
        pass_b(3)
        a_pass(1)
        a_own(3)
        far_pass(0)
        far_pass(1)
        a_pass(2)
        pass_b(4)
        pass_b(5)
        far_copy(1, 0, True).wait_recv()
        far_copy(1, 1, True).wait_recv()
        far_b(0)
        far_b(1)
        far_steps(FAR_ORDER[0:4])
        a_pass(3)
        far_pass(2)
        pass_b(6)
        far_b(2)
        far_steps(FAR_ORDER[4:6])
        far_pass(3)
        pass_b(7)
        far_copy(1, 2, True).wait_recv()
        far_steps(FAR_ORDER[6:9])
        far_copy(1, 3, True).wait_recv()
        far_steps(FAR_ORDER[9:12])
        far_b(3)
        far_steps(FAR_ORDER[12:16])
        for i in range(PARTS):
            a_done(i)
            for s in range(rows_n):
                order(s, i)
        send_partial(0, rows_n)
        part = product(0, rows_n, r)

        def keep(i, carry):
            at, total = part(i)
            for p in range(steps):
                fp_out[i, p] = total[:, p * TS : (p + 1) * TS]
            return carry

        for i, p in FAR_ORDER:
            fp_copy(i, p).wait_send()
        lax.fori_loop(0, PARTS, keep, 0)
        swap().wait_recv()

        def stay(i, carry):
            at = pl.ds(pl.multiple_of(i * ra, ra), ra)
            for p in range(steps):
                cols = pl.ds(p * TS, TS)
                out_ref[at, cols] = (fp_out[i, p] + part_in[at, cols]).astype(jnp.bfloat16)
            return carry

        lax.fori_loop(0, PARTS, stay, 0)
        for i, p in FAR_ORDER:
            f_copy(i, p).wait_send()
        for i in range(PARTS):
            far_copy(1, i).wait_send()
        for j in range(chunks):
            b_copy(1, j).wait_send()
            b_copy(2, j).wait_send()

    swap().wait_send()
    for i in range(PARTS):
        for kind in range(4):
            a_copy(kind, i).wait_send()
    for j in range(chunks):
        b_copy(0, j).wait_send()


FAR_ORDER = (
    (0, 0), (1, 0), (0, 1), (1, 1),
    (0, 2), (1, 2),
    (2, 0), (2, 1), (2, 2),
    (3, 0), (3, 1), (3, 2),
    (0, 3), (1, 3), (2, 3), (3, 3),
)


def fused(rows_n, cols_n, amplitudes, integrals, tile_mask, k_irrep, n_irrep, stored_tile):
    mrow, kcol = amplitudes.shape
    kb, ncol = integrals.shape
    half = ncol // 2
    steps = half // TS
    smem = pl.BlockSpec(memory_space=pltpu.SMEM)
    vmem = pl.BlockSpec(memory_space=pltpu.VMEM)
    tiles = pltpu.VMEM((PARTS, steps, mrow // PARTS, TS), jnp.float32)
    chunk = pltpu.VMEM((cols_n * kcol // TS, mrow // PARTS, TS), jnp.bfloat16)
    dma = pltpu.SemaphoreType.DMA
    return pl.pallas_call(
        kernel,
        out_shape=jax.ShapeDtypeStruct((mrow, half), jnp.bfloat16),
        in_specs=[pl.BlockSpec(memory_space=pl.ANY), vmem, smem, smem, smem, smem],
        out_specs=vmem,
        scratch_shapes=[
            chunk,
            chunk,
            chunk,
            chunk,
            pltpu.VMEM((rows_n, mrow, kb), jnp.bfloat16),
            pltpu.VMEM((2, mrow, kb), jnp.bfloat16),
            pltpu.VMEM((rows_n, kb, ncol), jnp.bfloat16),
            pltpu.VMEM((mrow, half), jnp.float32),
            pltpu.VMEM((mrow, half), jnp.float32),
            tiles,
            tiles,
            tiles,
            dma((PARTS, kcol // TS)),
            dma((4, PARTS)),
            dma((4, PARTS)),
            dma((3, 2 * steps)),
            dma((3, 2 * steps)),
            dma((2, PARTS)),
            dma((2, PARTS)),
            dma((PARTS, steps)),
            dma((PARTS, steps)),
            dma((PARTS, steps)),
            dma((PARTS, steps)),
            dma((1,)),
            dma((1,)),
        ],
        compiler_params=pltpu.CompilerParams(
            collective_id=0, has_side_effects=True, vmem_limit_bytes=56 << 20
        ),
        cost_estimate=pl.CostEstimate(
            flops=2 * mrow * kb * rows_n * ncol,
            bytes_accessed=2 * (mrow * kcol + kb * ncol + mrow * half),
            transcendentals=0,
        ),
    )(amplitudes, integrals, tile_mask, k_irrep, n_irrep, stored_tile)


def gathered_form(amplitudes, integrals, tile_mask, k_irrep, n_irrep, stored_tile):
    slab = lax.axis_index("rep")
    column = lax.axis_index("col")
    place = lax.axis_index("row")
    kb, ncol = integrals.shape
    tiles_col = ncol // TS
    own = kb // TS
    slab_tiles = own * lax.axis_size("row")
    n_labels = lax.dynamic_slice_in_dim(n_irrep, column * tiles_col, tiles_col)
    mask_cols = lax.dynamic_slice_in_dim(tile_mask, column * tiles_col, tiles_col, 1)
    slots = lax.dynamic_slice_in_dim(stored_tile, slab * slab_tiles, slab_tiles)
    mine = lax.dynamic_slice_in_dim(slots, place * own, own)
    same = jnp.take(k_irrep, mine)[:, None] == n_labels[None, :]
    weights = jnp.logical_and(same, jnp.take(mask_cols, mine, axis=0) == 1).astype(jnp.bfloat16)
    shaped = integrals.reshape(own, TS, tiles_col, TS) * weights[:, None, :, None]
    masked = lax.all_gather(shaped.reshape(kb, ncol), "row", axis=0, tiled=True)
    amp_slab = lax.all_gather(amplitudes, "col", axis=1, tiled=True)
    mrow, kq = amp_slab.shape
    ordered = jnp.take(
        amp_slab.reshape(mrow, slab_tiles, TS), slots - slab * slab_tiles, axis=1
    ).reshape(mrow, kq)
    partial_value = jnp.dot(ordered, masked, preferred_element_type=jnp.float32)
    return lax.psum_scatter(partial_value, "rep", scatter_dimension=1, tiled=True).astype(
        jnp.bfloat16
    )


def solution(mesh):
    rows_n, cols_n, reps = (mesh.shape[name] for name in ("row", "col", "rep"))
    if (rows_n, cols_n, reps) == (4, 4, 2):
        body = functools.partial(fused, rows_n, cols_n)
    else:
        body = gathered_form
    placed = (P("row", ("rep", "col")), P(("rep", "row"), "col"), P(), P(), P(), P())
    return jax.shard_map(
        body, mesh=mesh, in_specs=placed, out_specs=P("row", ("col", "rep")), check_vma=False
    )
```

```python
import functools

import jax
import jax.numpy as jnp
from jax import lax
from jax.experimental import pallas as pl
from jax.experimental.pallas import tpu as pltpu
from jax.sharding import PartitionSpec as P

TS = 128
PARTS = 4


def remote(src, dst, send_sem, recv_sem, **target):
    return pltpu.make_async_remote_copy(
        src_ref=src,
        dst_ref=dst,
        send_sem=send_sem,
        recv_sem=recv_sem,
        device_id=target,
        device_id_type=pl.DeviceIdType.MESH,
    )


def kernel(
    a_ref,
    b_ref,
    mask_ref,
    k_ref,
    n_ref,
    stored_ref,
    out_ref,
    a_0,
    a_1,
    a_2,
    a_3,
    a_ord,
    a_far,
    b_all,
    part_out,
    part_in,
    fp_out,
    f_in,
    f_out,
    own_sem,
    a_send,
    a_recv,
    b_send,
    b_recv,
    far_send,
    far_recv,
    fp_send,
    fp_recv,
    f_send,
    f_recv,
    p_send,
    p_recv,
):
    a_all = (a_0, a_1, a_2, a_3)
    z = lax.axis_index("row")
    c = lax.axis_index("col")
    r = lax.axis_index("rep")
    rows_n = b_all.shape[0]
    end = jnp.logical_or(z == 0, z == rows_n - 1)
    inner = jnp.logical_not(end)
    near = 2 * (z // 2)
    far = 2 - near
    buddy = z + 1 - 2 * (z % 2)
    across = rows_n - 1 - z
    beyond = rows_n - 1 - buddy
    x = c % 2
    y = c // 2
    xn = y * 2 + (1 - x)
    yn = (1 - y) * 2 + x
    diag = (1 - y) * 2 + (1 - x)
    mrow, kcol = a_ref.shape
    kb, ncol = b_ref.shape
    half = ncol // 2
    slots = kb // TS
    slab_tiles = slots * rows_n
    per = kcol // TS
    ra = mrow // PARTS
    steps = half // TS
    wide = half // 2
    mesh_id = pl.DeviceIdType.MESH

    own = [
        pltpu.make_async_copy(
            a_ref.at[pl.ds(i * ra, ra), pl.ds(t * TS, TS)],
            a_all[i].at[c * per + t],
            own_sem.at[i, t],
        )
        for i in range(PARTS)
        for t in range(per)
    ]
    for copy in own:
        copy.start()

    barrier = pltpu.get_barrier_semaphore()
    pl.semaphore_signal(barrier, inc=1, device_id={"col": xn}, device_id_type=mesh_id)
    pl.semaphore_signal(barrier, inc=1, device_id={"col": yn}, device_id_type=mesh_id)
    pl.semaphore_signal(barrier, inc=1, device_id={"rep": 1 - r}, device_id_type=mesh_id)
    pl.semaphore_signal(barrier, inc=1, device_id={"row": buddy}, device_id_type=mesh_id)

    @pl.when(inner)
    def _():
        pl.semaphore_signal(barrier, inc=1, device_id={"row": across}, device_id_type=mesh_id)

    pl.semaphore_wait(barrier, 4 + jnp.where(inner, 1, 0))

    for copy in own:
        copy.wait()

    def rows(i):
        return pl.ds(i * ra, ra)

    def a_copy(kind, i, receive=False):
        link = kind % 2
        if kind < 2:
            owner = (xn, yn)[link] if receive else c
            view = a_all[i].at[pl.ds(owner * per, per)]
        else:
            owner = diag if receive else (yn, xn)[link]
            part = pl.ds(link * (ra // 2), ra // 2)
            view = a_all[i].at[pl.ds(owner * per, per), part, :]
        return remote(view, view, a_send.at[kind, i], a_recv.at[kind, i], col=(xn, yn)[link])

    def a_own(i):
        if i < PARTS:
            a_copy(0, i).start()
            a_copy(1, i).start()

    def a_pass(i):
        a_copy(0, i, True).wait_recv()
        a_copy(3, i).start()
        a_copy(1, i, True).wait_recv()
        a_copy(2, i).start()

    def a_done(i):
        a_copy(2, i, True).wait_recv()
        a_copy(3, i, True).wait_recv()

    def tile_of(j):
        p = j // 2
        return ((1 - r) if j % 2 == 0 else r) * steps + p

    def lanes(t):
        return pl.ds(pl.multiple_of(t * TS, TS), TS)

    def b_copy(kind, j, receive=False):
        if receive:
            owner = (buddy, across, beyond, beyond, across)[kind]
        else:
            owner = (z, z, buddy, across, beyond)[kind]
        view = b_all.at[owner, :, lanes(tile_of(j))]
        target = across if kind in (1, 2) else buddy
        return remote(view, view, b_send.at[kind, j], b_recv.at[kind, j], row=target)

    def far_copy(kind, i, h, receive=False):
        side = (x, y)[h]
        at = pl.ds(i * ra + h * (ra // 2), ra // 2)
        if kind == 0:
            src = a_far.at[side, at, :] if receive else a_ord.at[far + side, at, :]
            dst = a_far.at[side, at, :]
            return remote(src, dst, far_send.at[0, i, h], far_recv.at[0, i, h], row=buddy)
        view = a_far.at[(1 - side) if receive else side, at, :]
        return remote(
            view, view, far_send.at[1, i, h], far_recv.at[1, i, h], col=(xn, yn)[h]
        )

    def fp_copy(i, p):
        return remote(
            fp_out.at[i, p], f_in.at[i, p], fp_send.at[i, p], fp_recv.at[i, p], rep=1 - r
        )

    def f_copy(i, p):
        return remote(
            f_out.at[i, p], f_in.at[i, p], f_send.at[i, p], f_recv.at[i, p], row=buddy
        )

    def swap(h):
        return remote(part_out.at[h], part_in.at[h], p_send.at[h], p_recv.at[h], rep=1 - r)

    def order(block, i):
        def one(s, carry):
            t = jnp.maximum(stored_ref[r * slab_tiles + block * slots + s] - r * slab_tiles, 0)
            a_ord[block, rows(i), lanes(s)] = a_all[i][t]
            return carry

        lax.fori_loop(0, slots, one, 0)

    def mask(j):
        tile = tile_of(j)
        g = c * (ncol // TS) + tile

        def one(t, carry):
            k = stored_ref[r * slab_tiles + z * slots + t]
            ok = jnp.logical_and(k_ref[k] == n_ref[g], mask_ref[k, g] == 1)
            weight = jnp.where(ok, 1.0, 0.0).astype(jnp.float32)
            at = pl.ds(pl.multiple_of(t * TS, TS), TS)
            value = b_ref[at, lanes(tile)].astype(jnp.float32) * weight
            b_all[z, at, lanes(tile)] = value.astype(jnp.bfloat16)
            return carry

        lax.fori_loop(0, slots, one, 0)

    def product(first, count, side, h, extra=False):
        cols = pl.ds(pl.multiple_of(side * half + h * wide, wide), wide)

        def one(i):
            at = pl.ds(pl.multiple_of(i * ra, ra), ra)
            total = jnp.zeros((ra, wide), jnp.float32)
            for s in range(count):
                total += jnp.dot(
                    a_ord[first + s, at, :],
                    b_all[first + s, :, cols],
                    preferred_element_type=jnp.float32,
                )
            if not extra:
                return at, total
            more = jnp.zeros((ra, TS), jnp.float32)
            for s in range(2):
                more += jnp.dot(
                    a_ord[far + s, at, :],
                    b_all[far + s, :, lanes(side * steps)],
                    preferred_element_type=jnp.float32,
                )
            return at, jnp.concatenate([total[:, :TS] + more, total[:, TS:]], axis=1)

        return one

    def send_partial(first, count, h, extra=False):
        part = product(first, count, 1 - r, h, extra)

        def away(i, carry):
            at, total = part(i)
            part_out[h, at, :] = total
            return carry

        lax.fori_loop(0, PARTS, away, 0)
        swap(h).start()

    def far_dot(i, j):
        total = jnp.zeros((ra, TS), jnp.float32)
        for s in range(2):
            total += jnp.dot(
                a_far[s, rows(i), :],
                b_all[far + s, :, lanes(tile_of(j))],
                preferred_element_type=jnp.float32,
            )
        return total

    def far_steps(pairs):
        for i, p in pairs:
            fp_out[i, p] = far_dot(i, 2 * p)
            fp_copy(i, p).start()
        for i, p in pairs:
            total = far_dot(i, 2 * p + 1)
            fp_copy(i, p).wait_recv()
            f_out[i, p] = total + f_in[i, p]
            f_copy(i, p).start()

    a_own(0)
    a_own(1)
    chunks = 2 * steps

    @pl.when(end)
    def _():
        sent = PARTS + 1
        for j in range(chunks):
            mask(j)
            if j < sent:
                b_copy(0, j).start()
        for i in range(PARTS):
            a_pass(i)
            a_own(i + 2)
            a_done(i)
            order(far, i)
            order(far + 1, i)
            for h in range(2):
                far_copy(0, i, h).start()
            upto = min(chunks, sent + i + 1)
            for j in range(sent, upto):
                b_copy(0, j).start()
            sent = upto
        for i in range(PARTS):
            order(near, i)
            order(near + 1, i)
        for j in range(chunks):
            b_copy(0, j, True).wait_recv()
        for h in (1, 0):
            if h == 0:
                for j in range(2):
                    b_copy(3, j, True).wait_recv()
                    b_copy(4, j, True).wait_recv()
            send_partial(near, 2, h, h == 0)
            part = product(near, 2, r, h, h == 0)

            def stay(i, carry, part=part, h=h):
                at, total = part(i)
                for p in range(2):
                    f_out[i, 2 * h + p] = total[:, p * TS : (p + 1) * TS]
                return carry

            lax.fori_loop(0, PARTS, stay, 0)
        swap(1).wait_recv()
        swap(0).wait_recv()

        def place(i, p, extra):
            value = f_out[i, p] + part_in[p // 2, rows(i), pl.ds((p % 2) * TS, TS)]
            if extra:
                value = value + f_in[i, p]
            out_ref[rows(i), pl.ds(p * TS, TS)] = value.astype(jnp.bfloat16)

        for i in range(PARTS):
            place(i, 0, False)
        for i, p in FAR_ORDER:
            f_copy(i, p).wait_recv()
            place(i, p, True)
        for i in range(PARTS):
            for h in range(2):
                far_copy(0, i, h).wait_send()

    @pl.when(inner)
    def _():
        def pass_b(j):
            b_copy(1, j).start()
            b_copy(0, j, True).wait_recv()
            b_copy(2, j).start()

        def far_pass(i):
            for h in range(2):
                far_copy(0, i, h, True).wait_recv()
                far_copy(1, i, h).start()

        def far_got(i):
            for h in range(2):
                far_copy(1, i, h, True).wait_recv()

        def far_b(p):
            for j in (2 * p, 2 * p + 1):
                b_copy(1, j, True).wait_recv()
                b_copy(2, j, True).wait_recv()

        for j in range(chunks):
            mask(j)
            b_copy(0, j).start()
        pass_b(0)
        pass_b(1)
        a_pass(0)
        a_own(2)
        pass_b(2)
        pass_b(3)
        a_pass(1)
        a_own(3)
        pass_b(4)
        far_b(0)
        for j in range(2):
            b_copy(3, j).start()
            b_copy(4, j).start()
        far_pass(0)
        a_pass(2)
        pass_b(5)
        far_pass(1)
        a_pass(3)
        pass_b(6)
        pass_b(7)
        far_b(1)
        far_got(0)
        far_got(1)
        far_steps(FAR_ORDER[0:2])
        far_b(2)
        far_steps(FAR_ORDER[2:4])
        for i in range(PARTS):
            a_done(i)
            for s in range(rows_n):
                order(s, i)
        far_pass(2)
        send_partial(0, rows_n, 0)
        part = product(0, rows_n, r, 0)

        def keep(i, carry):
            _, total = part(i)
            fp_out[i, 0] = total[:, :TS]
            f_out[i, 0] = total[:, TS:]
            return carry

        lax.fori_loop(0, PARTS, keep, 0)
        far_got(2)
        far_steps(FAR_ORDER[4:6])
        far_pass(3)
        far_b(3)
        far_steps(FAR_ORDER[6:9])
        far_got(3)
        far_steps(FAR_ORDER[9:12])
        send_partial(0, rows_n, 1)
        swap(0).wait_recv()
        for i in range(PARTS):
            for p in range(2):
                own_part = (fp_out, f_out)[p][i, 0]
                cols = pl.ds(p * TS, TS)
                out_ref[rows(i), cols] = (own_part + part_in[0, rows(i), cols]).astype(
                    jnp.bfloat16
                )
        swap(1).wait_recv()
        part1 = product(0, rows_n, r, 1)

        def stay(i, carry):
            at, total = part1(i)
            out_ref[at, pl.ds(wide, wide)] = (total + part_in[1, at, :]).astype(jnp.bfloat16)
            return carry

        lax.fori_loop(0, PARTS, stay, 0)
        for i, p in FAR_ORDER:
            fp_copy(i, p).wait_send()
            f_copy(i, p).wait_send()
        for i in range(PARTS):
            for h in range(2):
                far_copy(1, i, h).wait_send()
        for j in range(chunks):
            b_copy(1, j).wait_send()
            b_copy(2, j).wait_send()
        for j in range(2):
            b_copy(3, j).wait_send()
            b_copy(4, j).wait_send()

    for h in range(2):
        swap(h).wait_send()
    for i in range(PARTS):
        for kind in range(4):
            a_copy(kind, i).wait_send()
    for j in range(chunks):
        b_copy(0, j).wait_send()


FAR_ORDER = (
    (0, 1), (1, 1), (0, 2), (1, 2),
    (2, 1), (2, 2),
    (0, 3), (1, 3), (2, 3),
    (3, 1), (3, 2), (3, 3),
)


def fused(rows_n, cols_n, amplitudes, integrals, tile_mask, k_irrep, n_irrep, stored_tile):
    mrow, kcol = amplitudes.shape
    kb, ncol = integrals.shape
    half = ncol // 2
    steps = half // TS
    smem = pl.BlockSpec(memory_space=pltpu.SMEM)
    vmem = pl.BlockSpec(memory_space=pltpu.VMEM)
    tiles = pltpu.VMEM((PARTS, steps, mrow // PARTS, TS), jnp.float32)
    chunk = pltpu.VMEM((cols_n * kcol // TS, mrow // PARTS, TS), jnp.bfloat16)
    dma = pltpu.SemaphoreType.DMA
    return pl.pallas_call(
        kernel,
        out_shape=jax.ShapeDtypeStruct((mrow, half), jnp.bfloat16),
        in_specs=[pl.BlockSpec(memory_space=pl.ANY), vmem, smem, smem, smem, smem],
        out_specs=vmem,
        scratch_shapes=[
            chunk,
            chunk,
            chunk,
            chunk,
            pltpu.VMEM((rows_n, mrow, kb), jnp.bfloat16),
            pltpu.VMEM((2, mrow, kb), jnp.bfloat16),
            pltpu.VMEM((rows_n, kb, ncol), jnp.bfloat16),
            pltpu.VMEM((2, mrow, half // 2), jnp.float32),
            pltpu.VMEM((2, mrow, half // 2), jnp.float32),
            tiles,
            tiles,
            tiles,
            dma((PARTS, kcol // TS)),
            dma((4, PARTS)),
            dma((4, PARTS)),
            dma((5, 2 * steps)),
            dma((5, 2 * steps)),
            dma((2, PARTS, 2)),
            dma((2, PARTS, 2)),
            dma((PARTS, steps)),
            dma((PARTS, steps)),
            dma((PARTS, steps)),
            dma((PARTS, steps)),
            dma((2,)),
            dma((2,)),
        ],
        compiler_params=pltpu.CompilerParams(
            collective_id=0, has_side_effects=True, vmem_limit_bytes=56 << 20
        ),
        cost_estimate=pl.CostEstimate(
            flops=2 * mrow * kb * rows_n * ncol,
            bytes_accessed=2 * (mrow * kcol + kb * ncol + mrow * half),
            transcendentals=0,
        ),
    )(amplitudes, integrals, tile_mask, k_irrep, n_irrep, stored_tile)


def gathered_form(amplitudes, integrals, tile_mask, k_irrep, n_irrep, stored_tile):
    slab = lax.axis_index("rep")
    column = lax.axis_index("col")
    place = lax.axis_index("row")
    kb, ncol = integrals.shape
    tiles_col = ncol // TS
    own = kb // TS
    slab_tiles = own * lax.axis_size("row")
    n_labels = lax.dynamic_slice_in_dim(n_irrep, column * tiles_col, tiles_col)
    mask_cols = lax.dynamic_slice_in_dim(tile_mask, column * tiles_col, tiles_col, 1)
    slots = lax.dynamic_slice_in_dim(stored_tile, slab * slab_tiles, slab_tiles)
    mine = lax.dynamic_slice_in_dim(slots, place * own, own)
    same = jnp.take(k_irrep, mine)[:, None] == n_labels[None, :]
    weights = jnp.logical_and(same, jnp.take(mask_cols, mine, axis=0) == 1).astype(jnp.bfloat16)
    shaped = integrals.reshape(own, TS, tiles_col, TS) * weights[:, None, :, None]
    masked = lax.all_gather(shaped.reshape(kb, ncol), "row", axis=0, tiled=True)
    amp_slab = lax.all_gather(amplitudes, "col", axis=1, tiled=True)
    mrow, kq = amp_slab.shape
    ordered = jnp.take(
        amp_slab.reshape(mrow, slab_tiles, TS), slots - slab * slab_tiles, axis=1
    ).reshape(mrow, kq)
    partial_value = jnp.dot(ordered, masked, preferred_element_type=jnp.float32)
    return lax.psum_scatter(partial_value, "rep", scatter_dimension=1, tiled=True).astype(
        jnp.bfloat16
    )


def solution(mesh):
    rows_n, cols_n, reps = (mesh.shape[name] for name in ("row", "col", "rep"))
    if (rows_n, cols_n, reps) == (4, 4, 2):
        body = functools.partial(fused, rows_n, cols_n)
    else:
        body = gathered_form
    placed = (P("row", ("rep", "col")), P(("rep", "row"), "col"), P(), P(), P(), P())
    return jax.shard_map(
        body, mesh=mesh, in_specs=placed, out_specs=P("row", ("col", "rep")), check_vma=False
    )
```

```python
import functools

import jax
import jax.numpy as jnp
from jax import lax
from jax.experimental import pallas as pl
from jax.experimental.pallas import tpu as pltpu
from jax.sharding import PartitionSpec as P

TS = 128
PARTS = 4
SPLIT = 5


def remote(src, dst, send_sem, recv_sem, **target):
    return pltpu.make_async_remote_copy(
        src_ref=src,
        dst_ref=dst,
        send_sem=send_sem,
        recv_sem=recv_sem,
        device_id=target,
        device_id_type=pl.DeviceIdType.MESH,
    )


def kernel(
    a_ref,
    b_ref,
    mask_ref,
    k_ref,
    n_ref,
    stored_ref,
    out_ref,
    a_0,
    a_1,
    a_2,
    a_3,
    a_4,
    a_ord,
    a_far,
    b_all,
    part_out,
    part_in,
    fp_out,
    f_in,
    f_out,
    acc,
    own_sem,
    a_send,
    a_recv,
    b_send,
    b_recv,
    far_send,
    far_recv,
    fp_send,
    fp_recv,
    f_send,
    f_recv,
    p_send,
    p_recv,
):
    a_all = (a_0, a_1, a_2, a_3, a_4)
    z = lax.axis_index("row")
    c = lax.axis_index("col")
    r = lax.axis_index("rep")
    rows_n = b_all.shape[0]
    end = jnp.logical_or(z == 0, z == rows_n - 1)
    inner = jnp.logical_not(end)
    near = 2 * (z // 2)
    far = 2 - near
    buddy = z + 1 - 2 * (z % 2)
    across = rows_n - 1 - z
    beyond = rows_n - 1 - buddy
    x = c % 2
    y = c // 2
    xn = y * 2 + (1 - x)
    yn = (1 - y) * 2 + x
    diag = (1 - y) * 2 + (1 - x)
    mrow, kcol = a_ref.shape
    kb, ncol = b_ref.shape
    half = ncol // 2
    slots = kb // TS
    slab_tiles = slots * rows_n
    per = kcol // TS
    ra = mrow // PARTS
    steps = half // TS
    wide = half // 2
    mesh_id = pl.DeviceIdType.MESH

    def size(i):
        return ra if i < PARTS - 1 else ra // 2

    def start(i):
        return i * ra if i < PARTS else i * ra - ra // 2

    def rows(i):
        return pl.ds(start(i), size(i))

    own = [
        pltpu.make_async_copy(
            a_ref.at[rows(i), pl.ds(t * TS, TS)],
            a_all[i].at[c * per + t],
            own_sem.at[i, t],
        )
        for i in range(SPLIT)
        for t in range(per)
    ]
    for copy in own:
        copy.start()

    barrier = pltpu.get_barrier_semaphore()
    pl.semaphore_signal(barrier, inc=1, device_id={"col": xn}, device_id_type=mesh_id)
    pl.semaphore_signal(barrier, inc=1, device_id={"col": yn}, device_id_type=mesh_id)
    pl.semaphore_signal(barrier, inc=1, device_id={"rep": 1 - r}, device_id_type=mesh_id)
    pl.semaphore_signal(barrier, inc=1, device_id={"row": buddy}, device_id_type=mesh_id)

    @pl.when(inner)
    def _():
        pl.semaphore_signal(barrier, inc=1, device_id={"row": across}, device_id_type=mesh_id)

    def a_copy(kind, i, receive=False):
        link = kind % 2
        if kind < 2:
            owner = (xn, yn)[link] if receive else c
            view = a_all[i].at[pl.ds(owner * per, per)]
        else:
            owner = diag if receive else (yn, xn)[link]
            part = pl.ds(link * (size(i) // 2), size(i) // 2)
            view = a_all[i].at[pl.ds(owner * per, per), part, :]
        return remote(view, view, a_send.at[kind, i], a_recv.at[kind, i], col=(xn, yn)[link])

    def a_own(i):
        if i < SPLIT:
            a_copy(0, i).start()
            a_copy(1, i).start()

    def a_pass(i):
        a_copy(0, i, True).wait_recv()
        a_copy(3, i).start()
        a_copy(1, i, True).wait_recv()
        a_copy(2, i).start()

    def a_done(i):
        a_copy(2, i, True).wait_recv()
        a_copy(3, i, True).wait_recv()

    def tile_of(j):
        p = j // 2
        return ((1 - r) if j % 2 == 0 else r) * steps + p

    def lanes(t):
        return pl.ds(pl.multiple_of(t * TS, TS), TS)

    def b_copy(kind, j, receive=False):
        if receive:
            owner = (buddy, across, beyond, beyond, across)[kind]
        else:
            owner = (z, z, buddy, across, beyond)[kind]
        view = b_all.at[owner, :, lanes(tile_of(j))]
        target = across if kind in (1, 2) else buddy
        return remote(view, view, b_send.at[kind, j], b_recv.at[kind, j], row=target)

    def far_copy(kind, i, h, receive=False):
        side = (x, y)[h]
        at = pl.ds(start(i) + h * (size(i) // 2), size(i) // 2)
        if kind == 0:
            src = a_far.at[side, at, :] if receive else a_ord.at[far + side, at, :]
            dst = a_far.at[side, at, :]
            return remote(src, dst, far_send.at[0, i, h], far_recv.at[0, i, h], row=buddy)
        view = a_far.at[(1 - side) if receive else side, at, :]
        return remote(
            view, view, far_send.at[1, i, h], far_recv.at[1, i, h], col=(xn, yn)[h]
        )

    def piece(ref, i, p):
        return ref.at[i, p, pl.ds(0, size(i))]

    def fp_copy(i, p):
        return remote(
            piece(fp_out, i, p), piece(f_in, i, p), fp_send.at[i, p], fp_recv.at[i, p], rep=1 - r
        )

    def f_copy(i, p):
        return remote(
            piece(f_out, i, p), piece(f_in, i, p), f_send.at[i, p], f_recv.at[i, p], row=buddy
        )

    def swap(h):
        return remote(part_out.at[h], part_in.at[h], p_send.at[h], p_recv.at[h], rep=1 - r)

    def order(block, i):
        def one(s, carry):
            t = jnp.maximum(stored_ref[r * slab_tiles + block * slots + s] - r * slab_tiles, 0)
            a_ord[block, rows(i), lanes(s)] = a_all[i][t]
            return carry

        lax.fori_loop(0, slots, one, 0)

    def mask(j):
        tile = tile_of(j)
        g = c * (ncol // TS) + tile

        def one(t, carry):
            k = stored_ref[r * slab_tiles + z * slots + t]
            ok = jnp.logical_and(k_ref[k] == n_ref[g], mask_ref[g, k] == 1)
            weight = jnp.where(ok, 1.0, 0.0).astype(jnp.float32)
            at = pl.ds(pl.multiple_of(t * TS, TS), TS)
            value = b_ref[at, lanes(tile)].astype(jnp.float32) * weight
            b_all[z, at, lanes(tile)] = value.astype(jnp.bfloat16)
            return carry

        lax.fori_loop(0, slots, one, 0)

    def product(first, count, side, h, extra=False):
        cols = pl.ds(pl.multiple_of(side * half + h * wide, wide), wide)

        def one(i):
            at = pl.ds(pl.multiple_of(i * ra, ra), ra)
            total = jnp.zeros((ra, wide), jnp.float32)
            for s in range(count):
                total += jnp.dot(
                    a_ord[first + s, at, :],
                    b_all[first + s, :, cols],
                    preferred_element_type=jnp.float32,
                )
            if not extra:
                return at, total
            more = jnp.zeros((ra, TS), jnp.float32)
            for s in range(2):
                more += jnp.dot(
                    a_ord[far + s, at, :],
                    b_all[far + s, :, lanes(side * steps)],
                    preferred_element_type=jnp.float32,
                )
            return at, jnp.concatenate([total[:, :TS] + more, total[:, TS:]], axis=1)

        return one

    def send_partial(first, count, h, extra=False):
        part = product(first, count, 1 - r, h, extra)

        def away(i, carry):
            at, total = part(i)
            part_out[h, at, :] = total
            return carry

        lax.fori_loop(0, PARTS, away, 0)
        swap(h).start()

    def far_dot(i, j):
        total = jnp.zeros((size(i), TS), jnp.float32)
        for s in range(2):
            total += jnp.dot(
                a_far[s, rows(i), :],
                b_all[far + s, :, lanes(tile_of(j))],
                preferred_element_type=jnp.float32,
            )
        return total

    def far_steps(pairs):
        for i, p in pairs:
            piece(fp_out, i, p)[...] = far_dot(i, 2 * p)
            fp_copy(i, p).start()
        for i, p in pairs:
            total = far_dot(i, 2 * p + 1)
            fp_copy(i, p).wait_recv()
            piece(f_out, i, p)[...] = total + piece(f_in, i, p)[...]
            f_copy(i, p).start()

    chunks = 2 * steps
    for j in range(PARTS):
        mask(j)
    pl.semaphore_wait(barrier, 4 + jnp.where(inner, 1, 0))
    for j in range(PARTS):
        b_copy(0, j).start()
    for copy in own:
        copy.wait()
    a_own(0)
    a_own(1)
    for j in range(PARTS, chunks):
        mask(j)

    @pl.when(end)
    def _():
        sent = PARTS + 1
        b_copy(0, PARTS).start()
        for i in range(SPLIT):
            a_pass(i)
            a_own(i + 2)
            a_done(i)
            order(far, i)
            order(far + 1, i)
            for h in range(2):
                far_copy(0, i, h).start()
            upto = min(chunks, sent + i + 1)
            for j in range(sent, upto):
                b_copy(0, j).start()
            sent = upto
        for i in range(SPLIT):
            order(near, i)
            order(near + 1, i)
        for j in range(chunks):
            b_copy(0, j, True).wait_recv()
        for h in (1, 0):
            if h == 0:
                for j in range(2):
                    b_copy(3, j, True).wait_recv()
                    b_copy(4, j, True).wait_recv()
            send_partial(near, 2, h, h == 0)
            part = product(near, 2, r, h, h == 0)

            def stay(i, carry, part=part, h=h):
                at, total = part(i)
                acc[at, pl.ds(h * wide, wide)] = total
                return carry

            lax.fori_loop(0, PARTS, stay, 0)
        swap(1).wait_recv()
        swap(0).wait_recv()

        def place(i, p, extra):
            value = acc[rows(i), pl.ds(p * TS, TS)]
            value = value + part_in[p // 2, rows(i), pl.ds((p % 2) * TS, TS)]
            if extra:
                value = value + piece(f_in, i, p)[...]
            out_ref[rows(i), pl.ds(p * TS, TS)] = value.astype(jnp.bfloat16)

        for i in range(SPLIT):
            place(i, 0, False)
        for i, p in FAR_ORDER:
            f_copy(i, p).wait_recv()
            place(i, p, True)
        for i in range(SPLIT):
            for h in range(2):
                far_copy(0, i, h).wait_send()

    @pl.when(inner)
    def _():
        def pass_b(j):
            b_copy(1, j).start()
            b_copy(0, j, True).wait_recv()
            b_copy(2, j).start()

        def far_pass(i):
            for h in range(2):
                far_copy(0, i, h, True).wait_recv()
                far_copy(1, i, h).start()

        def far_got(i):
            for h in range(2):
                far_copy(1, i, h, True).wait_recv()

        def far_b(p):
            for j in (2 * p, 2 * p + 1):
                b_copy(1, j, True).wait_recv()
                b_copy(2, j, True).wait_recv()

        for j in range(PARTS, chunks):
            b_copy(0, j).start()
        pass_b(0)
        pass_b(1)
        a_pass(0)
        a_own(2)
        pass_b(2)
        pass_b(3)
        a_pass(1)
        a_own(3)
        pass_b(4)
        far_b(0)
        for j in range(2):
            b_copy(3, j).start()
            b_copy(4, j).start()
        far_pass(0)
        a_pass(2)
        a_own(4)
        pass_b(5)
        far_pass(1)
        a_pass(3)
        a_pass(4)
        pass_b(6)
        pass_b(7)
        far_b(1)
        far_got(0)
        far_got(1)
        far_steps(FAR_ORDER[0:2])
        far_b(2)
        far_steps(FAR_ORDER[2:4])
        for i in range(SPLIT):
            a_done(i)
            for s in range(rows_n):
                order(s, i)
        far_pass(2)
        send_partial(0, rows_n, 0)
        part = product(0, rows_n, r, 0)

        def keep(i, carry):
            at, total = part(i)
            acc[at, pl.ds(0, wide)] = total
            return carry

        lax.fori_loop(0, PARTS, keep, 0)
        far_got(2)
        far_steps(FAR_ORDER[4:6])
        far_pass(3)
        far_b(3)
        far_steps(FAR_ORDER[6:9])
        far_got(3)
        far_steps(FAR_ORDER[9:12])
        far_pass(4)
        far_got(4)
        far_steps(FAR_ORDER[12:15])
        send_partial(0, rows_n, 1)
        swap(0).wait_recv()
        out_ref[:, :wide] = (acc[:, :wide] + part_in[0]).astype(jnp.bfloat16)
        swap(1).wait_recv()
        part1 = product(0, rows_n, r, 1)

        def stay(i, carry):
            at, total = part1(i)
            out_ref[at, pl.ds(wide, wide)] = (total + part_in[1, at, :]).astype(jnp.bfloat16)
            return carry

        lax.fori_loop(0, PARTS, stay, 0)
        for i, p in FAR_ORDER:
            fp_copy(i, p).wait_send()
            f_copy(i, p).wait_send()
        for i in range(SPLIT):
            for h in range(2):
                far_copy(1, i, h).wait_send()
        for j in range(chunks):
            b_copy(1, j).wait_send()
            b_copy(2, j).wait_send()
        for j in range(2):
            b_copy(3, j).wait_send()
            b_copy(4, j).wait_send()

    for h in range(2):
        swap(h).wait_send()
    for i in range(SPLIT):
        for kind in range(4):
            a_copy(kind, i).wait_send()
    for j in range(chunks):
        b_copy(0, j).wait_send()


FAR_ORDER = (
    (0, 1), (1, 1), (0, 2), (1, 2),
    (2, 1), (2, 2),
    (0, 3), (1, 3), (2, 3),
    (3, 1), (3, 2), (3, 3),
    (4, 1), (4, 2), (4, 3),
)


def fused(rows_n, cols_n, amplitudes, integrals, tile_mask, k_irrep, n_irrep, stored_tile):
    mrow, kcol = amplitudes.shape
    kb, ncol = integrals.shape
    half = ncol // 2
    steps = half // TS
    smem = pl.BlockSpec(memory_space=pltpu.SMEM)
    vmem = pl.BlockSpec(memory_space=pltpu.VMEM)
    tiles = pltpu.VMEM((SPLIT, steps, mrow // PARTS, TS), jnp.float32)
    chunk = pltpu.VMEM((cols_n * kcol // TS, mrow // PARTS, TS), jnp.bfloat16)
    last = pltpu.VMEM((cols_n * kcol // TS, mrow // PARTS // 2, TS), jnp.bfloat16)
    dma = pltpu.SemaphoreType.DMA
    return pl.pallas_call(
        kernel,
        out_shape=jax.ShapeDtypeStruct((mrow, half), jnp.bfloat16),
        in_specs=[pl.BlockSpec(memory_space=pl.ANY), vmem, smem, smem, smem, smem],
        out_specs=vmem,
        scratch_shapes=[
            chunk,
            chunk,
            chunk,
            last,
            last,
            pltpu.VMEM((rows_n, mrow, kb), jnp.bfloat16),
            pltpu.VMEM((2, mrow, kb), jnp.bfloat16),
            pltpu.VMEM((rows_n, kb, ncol), jnp.bfloat16),
            pltpu.VMEM((2, mrow, half // 2), jnp.float32),
            pltpu.VMEM((2, mrow, half // 2), jnp.float32),
            tiles,
            tiles,
            tiles,
            pltpu.VMEM((mrow, half), jnp.float32),
            dma((SPLIT, kcol // TS)),
            dma((4, SPLIT)),
            dma((4, SPLIT)),
            dma((5, 2 * steps)),
            dma((5, 2 * steps)),
            dma((2, SPLIT, 2)),
            dma((2, SPLIT, 2)),
            dma((SPLIT, steps)),
            dma((SPLIT, steps)),
            dma((SPLIT, steps)),
            dma((SPLIT, steps)),
            dma((2,)),
            dma((2,)),
        ],
        compiler_params=pltpu.CompilerParams(
            collective_id=0, has_side_effects=True, vmem_limit_bytes=56 << 20
        ),
        cost_estimate=pl.CostEstimate(
            flops=2 * mrow * kb * rows_n * ncol,
            bytes_accessed=2 * (mrow * kcol + kb * ncol + mrow * half),
            transcendentals=0,
        ),
    )(amplitudes, integrals, tile_mask.T, k_irrep, n_irrep, stored_tile)


def gathered_form(amplitudes, integrals, tile_mask, k_irrep, n_irrep, stored_tile):
    slab = lax.axis_index("rep")
    column = lax.axis_index("col")
    place = lax.axis_index("row")
    kb, ncol = integrals.shape
    tiles_col = ncol // TS
    own = kb // TS
    slab_tiles = own * lax.axis_size("row")
    n_labels = lax.dynamic_slice_in_dim(n_irrep, column * tiles_col, tiles_col)
    mask_cols = lax.dynamic_slice_in_dim(tile_mask, column * tiles_col, tiles_col, 1)
    slots = lax.dynamic_slice_in_dim(stored_tile, slab * slab_tiles, slab_tiles)
    mine = lax.dynamic_slice_in_dim(slots, place * own, own)
    same = jnp.take(k_irrep, mine)[:, None] == n_labels[None, :]
    weights = jnp.logical_and(same, jnp.take(mask_cols, mine, axis=0) == 1).astype(jnp.bfloat16)
    shaped = integrals.reshape(own, TS, tiles_col, TS) * weights[:, None, :, None]
    masked = lax.all_gather(shaped.reshape(kb, ncol), "row", axis=0, tiled=True)
    amp_slab = lax.all_gather(amplitudes, "col", axis=1, tiled=True)
    mrow, kq = amp_slab.shape
    ordered = jnp.take(
        amp_slab.reshape(mrow, slab_tiles, TS), slots - slab * slab_tiles, axis=1
    ).reshape(mrow, kq)
    partial_value = jnp.dot(ordered, masked, preferred_element_type=jnp.float32)
    return lax.psum_scatter(partial_value, "rep", scatter_dimension=1, tiled=True).astype(
        jnp.bfloat16
    )


def solution(mesh):
    rows_n, cols_n, reps = (mesh.shape[name] for name in ("row", "col", "rep"))
    if (rows_n, cols_n, reps) == (4, 4, 2):
        body = functools.partial(fused, rows_n, cols_n)
    else:
        body = gathered_form
    placed = (P("row", ("rep", "col")), P(("rep", "row"), "col"), P(), P(), P(), P())
    return jax.shard_map(
        body, mesh=mesh, in_specs=placed, out_specs=P("row", ("col", "rep")), check_vma=False
    )
```

```python
import functools

import jax
import jax.numpy as jnp
from jax import lax
from jax.experimental import pallas as pl
from jax.experimental.pallas import tpu as pltpu
from jax.sharding import PartitionSpec as P

TS = 128
PARTS = 4
SPLIT = 5


def remote(src, dst, send_sem, recv_sem, **target):
    return pltpu.make_async_remote_copy(
        src_ref=src,
        dst_ref=dst,
        send_sem=send_sem,
        recv_sem=recv_sem,
        device_id=target,
        device_id_type=pl.DeviceIdType.MESH,
    )


def kernel(
    a_ref,
    b_ref,
    mask_ref,
    k_ref,
    n_ref,
    stored_ref,
    out_ref,
    a_0,
    a_1,
    a_2,
    a_3,
    a_4,
    a_ord,
    a_far,
    b_all,
    part_out,
    part_in,
    fp_out,
    f_in,
    f_out,
    acc,
    own_sem,
    a_send,
    a_recv,
    b_send,
    b_recv,
    far_send,
    far_recv,
    fp_send,
    fp_recv,
    f_send,
    f_recv,
    p_send,
    p_recv,
):
    a_all = (a_0, a_1, a_2, a_3, a_4)
    z = lax.axis_index("row")
    c = lax.axis_index("col")
    r = lax.axis_index("rep")
    rows_n = b_all.shape[0]
    end = jnp.logical_or(z == 0, z == rows_n - 1)
    inner = jnp.logical_not(end)
    near = 2 * (z // 2)
    far = 2 - near
    buddy = z + 1 - 2 * (z % 2)
    across = rows_n - 1 - z
    beyond = rows_n - 1 - buddy
    x = c % 2
    y = c // 2
    xn = y * 2 + (1 - x)
    yn = (1 - y) * 2 + x
    diag = (1 - y) * 2 + (1 - x)
    mrow, kcol = a_ref.shape
    kb, ncol = b_ref.shape
    half = ncol // 2
    slots = kb // TS
    slab_tiles = slots * rows_n
    per = kcol // TS
    ra = mrow // PARTS
    steps = half // TS
    wide = half // 2
    mesh_id = pl.DeviceIdType.MESH

    def size(i):
        return ra if i < PARTS - 1 else ra // 2

    def start(i):
        return i * ra if i < PARTS else i * ra - ra // 2

    def rows(i):
        return pl.ds(start(i), size(i))

    own = [
        pltpu.make_async_copy(
            a_ref.at[rows(i), pl.ds(t * TS, TS)],
            a_all[i].at[c * per + t],
            own_sem.at[i, t],
        )
        for i in range(SPLIT)
        for t in range(per)
    ]
    for copy in own:
        copy.start()

    barrier = pltpu.get_barrier_semaphore()
    pl.semaphore_signal(barrier, inc=1, device_id={"col": xn}, device_id_type=mesh_id)
    pl.semaphore_signal(barrier, inc=1, device_id={"col": yn}, device_id_type=mesh_id)
    pl.semaphore_signal(barrier, inc=1, device_id={"rep": 1 - r}, device_id_type=mesh_id)
    pl.semaphore_signal(barrier, inc=1, device_id={"row": buddy}, device_id_type=mesh_id)

    @pl.when(inner)
    def _():
        pl.semaphore_signal(barrier, inc=1, device_id={"row": across}, device_id_type=mesh_id)

    def a_copy(kind, i, receive=False):
        link = kind % 2
        if kind < 2:
            owner = (xn, yn)[link] if receive else c
            view = a_all[i].at[pl.ds(owner * per, per)]
        else:
            owner = diag if receive else (yn, xn)[link]
            part = pl.ds(link * (size(i) // 2), size(i) // 2)
            view = a_all[i].at[pl.ds(owner * per, per), part, :]
        return remote(view, view, a_send.at[kind, i], a_recv.at[kind, i], col=(xn, yn)[link])

    def a_own(i):
        if i < SPLIT:
            a_copy(0, i).start()
            a_copy(1, i).start()

    def a_pass(i):
        a_copy(0, i, True).wait_recv()
        a_copy(3, i).start()
        a_copy(1, i, True).wait_recv()
        a_copy(2, i).start()

    def a_done(i):
        a_copy(2, i, True).wait_recv()
        a_copy(3, i, True).wait_recv()

    def tile_of(j):
        p = j // 2
        return ((1 - r) if j % 2 == 0 else r) * steps + p

    def lanes(t):
        return pl.ds(pl.multiple_of(t * TS, TS), TS)

    def b_copy(kind, j, receive=False):
        if receive:
            owner = (buddy, across, beyond, beyond, across)[kind]
        else:
            owner = (z, z, buddy, across, beyond)[kind]
        view = b_all.at[owner, :, lanes(tile_of(j))]
        target = across if kind in (1, 2) else buddy
        return remote(view, view, b_send.at[kind, j], b_recv.at[kind, j], row=target)

    def far_copy(kind, i, h, receive=False):
        side = (x, y)[h]
        at = pl.ds(start(i) + h * (size(i) // 2), size(i) // 2)
        if kind == 0:
            src = a_far.at[side, at, :] if receive else a_ord.at[far + side, at, :]
            dst = a_far.at[side, at, :]
            return remote(src, dst, far_send.at[0, i, h], far_recv.at[0, i, h], row=buddy)
        view = a_far.at[(1 - side) if receive else side, at, :]
        return remote(
            view, view, far_send.at[1, i, h], far_recv.at[1, i, h], col=(xn, yn)[h]
        )

    def piece(ref, i, p):
        return ref.at[i, p, pl.ds(0, size(i))]

    def fp_copy(i, p):
        return remote(
            piece(fp_out, i, p), piece(f_in, i, p), fp_send.at[i, p], fp_recv.at[i, p], rep=1 - r
        )

    def f_copy(i, p):
        return remote(
            piece(f_out, i, p), piece(f_in, i, p), f_send.at[i, p], f_recv.at[i, p], row=buddy
        )

    def swap(h):
        return remote(part_out.at[h], part_in.at[h], p_send.at[h], p_recv.at[h], rep=1 - r)

    def order(block, i):
        def one(s, carry):
            t = jnp.maximum(stored_ref[r * slab_tiles + block * slots + s] - r * slab_tiles, 0)
            a_ord[block, rows(i), lanes(s)] = a_all[i][t]
            return carry

        lax.fori_loop(0, slots, one, 0)

    def mask(j):
        tile = tile_of(j)
        g = c * (ncol // TS) + tile

        def one(t, carry):
            k = stored_ref[r * slab_tiles + z * slots + t]
            ok = jnp.logical_and(k_ref[k] == n_ref[g], mask_ref[g, k] == 1)
            weight = jnp.where(ok, 1.0, 0.0).astype(jnp.float32)
            at = pl.ds(pl.multiple_of(t * TS, TS), TS)
            value = b_ref[at, lanes(tile)].astype(jnp.float32) * weight
            b_all[z, at, lanes(tile)] = value.astype(jnp.bfloat16)
            return carry

        lax.fori_loop(0, slots, one, 0)

    def product(first, count, side, h):
        cols = pl.ds(pl.multiple_of(side * half + h * wide, wide), wide)

        def one(i):
            at = pl.ds(pl.multiple_of(i * ra, ra), ra)
            total = jnp.zeros((ra, wide), jnp.float32)
            for s in range(count):
                total += jnp.dot(
                    a_ord[first + s, at, :],
                    b_all[first + s, :, cols],
                    preferred_element_type=jnp.float32,
                )
            return at, total

        return one

    def send_partial(first, count, h):
        part = product(first, count, 1 - r, h)

        def away(i, carry):
            at, total = part(i)
            part_out[h, at, :] = total
            return carry

        lax.fori_loop(0, PARTS, away, 0)
        swap(h).start()

    def far_dot(i, j):
        total = jnp.zeros((size(i), TS), jnp.float32)
        for s in range(2):
            total += jnp.dot(
                a_far[s, rows(i), :],
                b_all[far + s, :, lanes(tile_of(j))],
                preferred_element_type=jnp.float32,
            )
        return total

    def far_steps(pairs):
        for i, p in pairs:
            piece(fp_out, i, p)[...] = far_dot(i, 2 * p)
            fp_copy(i, p).start()
        for i, p in pairs:
            total = far_dot(i, 2 * p + 1)
            fp_copy(i, p).wait_recv()
            piece(f_out, i, p)[...] = total + piece(f_in, i, p)[...]
            f_copy(i, p).start()

    chunks = 2 * steps
    for j in range(PARTS):
        mask(j)
    pl.semaphore_wait(barrier, 4 + jnp.where(inner, 1, 0))
    for j in range(PARTS):
        b_copy(0, j).start()
    for copy in own:
        copy.wait()
    a_own(0)
    a_own(1)
    for j in range(PARTS, chunks):
        mask(j)

    @pl.when(end)
    def _():
        sent = PARTS + 2
        b_copy(0, PARTS).start()
        b_copy(0, PARTS + 1).start()
        for i in range(SPLIT):
            a_pass(i)
            a_own(i + 2)
            a_done(i)
            order(far, i)
            order(far + 1, i)
            for h in range(2):
                far_copy(0, i, h).start()
            upto = min(chunks, sent + 2)
            for j in range(sent, upto):
                b_copy(0, j).start()
            sent = upto
        for i in range(SPLIT):
            order(near, i)
            order(near + 1, i)
        for j in range(chunks):
            b_copy(0, j, True).wait_recv()
        for h in (1, 0):
            if h == 0:
                for j in range(PARTS):
                    b_copy(3, j, True).wait_recv()
                    b_copy(4, j, True).wait_recv()
            first, count = (0, rows_n) if h == 0 else (near, 2)
            send_partial(first, count, h)
            part = product(first, count, r, h)

            def stay(i, carry, part=part, h=h):
                at, total = part(i)
                acc[at, pl.ds(h * wide, wide)] = total
                return carry

            lax.fori_loop(0, PARTS, stay, 0)
        swap(1).wait_recv()
        swap(0).wait_recv()

        def place(i, p, extra):
            value = acc[rows(i), pl.ds(p * TS, TS)]
            value = value + part_in[p // 2, rows(i), pl.ds((p % 2) * TS, TS)]
            if extra:
                value = value + piece(f_in, i, p)[...]
            out_ref[rows(i), pl.ds(p * TS, TS)] = value.astype(jnp.bfloat16)

        for i in range(SPLIT):
            place(i, 0, False)
            place(i, 1, False)
        for i, p in FAR_ORDER:
            f_copy(i, p).wait_recv()
            place(i, p, True)
        for i in range(SPLIT):
            for h in range(2):
                far_copy(0, i, h).wait_send()

    @pl.when(inner)
    def _():
        def pass_b(j):
            b_copy(1, j).start()
            b_copy(0, j, True).wait_recv()
            b_copy(2, j).start()

        def far_pass(i):
            for h in range(2):
                far_copy(0, i, h, True).wait_recv()
                far_copy(1, i, h).start()

        def raw(p):
            for j in (2 * p, 2 * p + 1):
                b_copy(3, j).start()
                b_copy(4, j).start()

        def far_got(i):
            for h in range(2):
                far_copy(1, i, h, True).wait_recv()

        def far_b(p):
            for j in (2 * p, 2 * p + 1):
                b_copy(1, j, True).wait_recv()
                b_copy(2, j, True).wait_recv()

        for j in range(PARTS, chunks):
            b_copy(0, j).start()
        pass_b(0)
        pass_b(1)
        a_pass(0)
        a_own(2)
        pass_b(2)
        pass_b(3)
        a_pass(1)
        a_own(3)
        pass_b(4)
        far_b(0)
        raw(0)
        pass_b(5)
        a_pass(2)
        a_own(4)
        far_b(1)
        raw(1)
        far_pass(0)
        a_pass(3)
        pass_b(6)
        pass_b(7)
        a_pass(4)
        for i in range(SPLIT):
            a_done(i)
            for s in range(rows_n):
                order(s, i)
        far_pass(1)
        send_partial(0, rows_n, 0)
        part = product(0, rows_n, r, 0)

        def keep(i, carry):
            at, total = part(i)
            acc[at, pl.ds(0, wide)] = total
            return carry

        lax.fori_loop(0, PARTS, keep, 0)
        far_b(2)
        far_got(0)
        far_got(1)
        far_steps(FAR_ORDER[0:2])
        far_pass(2)
        far_pass(3)
        far_got(2)
        far_steps(FAR_ORDER[2:3])
        far_pass(4)
        far_b(3)
        far_steps(FAR_ORDER[3:6])
        far_got(3)
        far_got(4)
        far_steps(FAR_ORDER[6:10])
        send_partial(0, rows_n, 1)
        swap(0).wait_recv()
        out_ref[:, :wide] = (acc[:, :wide] + part_in[0]).astype(jnp.bfloat16)
        swap(1).wait_recv()
        part1 = product(0, rows_n, r, 1)

        def stay(i, carry):
            at, total = part1(i)
            out_ref[at, pl.ds(wide, wide)] = (total + part_in[1, at, :]).astype(jnp.bfloat16)
            return carry

        lax.fori_loop(0, PARTS, stay, 0)
        for i, p in FAR_ORDER:
            fp_copy(i, p).wait_send()
            f_copy(i, p).wait_send()
        for i in range(SPLIT):
            for h in range(2):
                far_copy(1, i, h).wait_send()
        for j in range(chunks):
            b_copy(1, j).wait_send()
            b_copy(2, j).wait_send()
        for j in range(PARTS):
            b_copy(3, j).wait_send()
            b_copy(4, j).wait_send()

    for h in range(2):
        swap(h).wait_send()
    for i in range(SPLIT):
        for kind in range(4):
            a_copy(kind, i).wait_send()
    for j in range(chunks):
        b_copy(0, j).wait_send()


FAR_ORDER = (
    (0, 2), (1, 2), (2, 2),
    (0, 3), (1, 3), (2, 3),
    (3, 2), (3, 3), (4, 2), (4, 3),
)


def fused(rows_n, cols_n, amplitudes, integrals, tile_mask, k_irrep, n_irrep, stored_tile):
    mrow, kcol = amplitudes.shape
    kb, ncol = integrals.shape
    half = ncol // 2
    steps = half // TS
    smem = pl.BlockSpec(memory_space=pltpu.SMEM)
    vmem = pl.BlockSpec(memory_space=pltpu.VMEM)
    tiles = pltpu.VMEM((SPLIT, steps, mrow // PARTS, TS), jnp.float32)
    chunk = pltpu.VMEM((cols_n * kcol // TS, mrow // PARTS, TS), jnp.bfloat16)
    last = pltpu.VMEM((cols_n * kcol // TS, mrow // PARTS // 2, TS), jnp.bfloat16)
    dma = pltpu.SemaphoreType.DMA
    return pl.pallas_call(
        kernel,
        out_shape=jax.ShapeDtypeStruct((mrow, half), jnp.bfloat16),
        in_specs=[pl.BlockSpec(memory_space=pl.ANY), vmem, smem, smem, smem, smem],
        out_specs=vmem,
        scratch_shapes=[
            chunk,
            chunk,
            chunk,
            last,
            last,
            pltpu.VMEM((rows_n, mrow, kb), jnp.bfloat16),
            pltpu.VMEM((2, mrow, kb), jnp.bfloat16),
            pltpu.VMEM((rows_n, kb, ncol), jnp.bfloat16),
            pltpu.VMEM((2, mrow, half // 2), jnp.float32),
            pltpu.VMEM((2, mrow, half // 2), jnp.float32),
            tiles,
            tiles,
            tiles,
            pltpu.VMEM((mrow, half), jnp.float32),
            dma((SPLIT, kcol // TS)),
            dma((4, SPLIT)),
            dma((4, SPLIT)),
            dma((5, 2 * steps)),
            dma((5, 2 * steps)),
            dma((2, SPLIT, 2)),
            dma((2, SPLIT, 2)),
            dma((SPLIT, steps)),
            dma((SPLIT, steps)),
            dma((SPLIT, steps)),
            dma((SPLIT, steps)),
            dma((2,)),
            dma((2,)),
        ],
        compiler_params=pltpu.CompilerParams(
            collective_id=0, has_side_effects=True, vmem_limit_bytes=56 << 20
        ),
        cost_estimate=pl.CostEstimate(
            flops=2 * mrow * kb * rows_n * ncol,
            bytes_accessed=2 * (mrow * kcol + kb * ncol + mrow * half),
            transcendentals=0,
        ),
    )(amplitudes, integrals, tile_mask.T, k_irrep, n_irrep, stored_tile)


def gathered_form(amplitudes, integrals, tile_mask, k_irrep, n_irrep, stored_tile):
    slab = lax.axis_index("rep")
    column = lax.axis_index("col")
    place = lax.axis_index("row")
    kb, ncol = integrals.shape
    tiles_col = ncol // TS
    own = kb // TS
    slab_tiles = own * lax.axis_size("row")
    n_labels = lax.dynamic_slice_in_dim(n_irrep, column * tiles_col, tiles_col)
    mask_cols = lax.dynamic_slice_in_dim(tile_mask, column * tiles_col, tiles_col, 1)
    slots = lax.dynamic_slice_in_dim(stored_tile, slab * slab_tiles, slab_tiles)
    mine = lax.dynamic_slice_in_dim(slots, place * own, own)
    same = jnp.take(k_irrep, mine)[:, None] == n_labels[None, :]
    weights = jnp.logical_and(same, jnp.take(mask_cols, mine, axis=0) == 1).astype(jnp.bfloat16)
    shaped = integrals.reshape(own, TS, tiles_col, TS) * weights[:, None, :, None]
    masked = lax.all_gather(shaped.reshape(kb, ncol), "row", axis=0, tiled=True)
    amp_slab = lax.all_gather(amplitudes, "col", axis=1, tiled=True)
    mrow, kq = amp_slab.shape
    ordered = jnp.take(
        amp_slab.reshape(mrow, slab_tiles, TS), slots - slab * slab_tiles, axis=1
    ).reshape(mrow, kq)
    partial_value = jnp.dot(ordered, masked, preferred_element_type=jnp.float32)
    return lax.psum_scatter(partial_value, "rep", scatter_dimension=1, tiled=True).astype(
        jnp.bfloat16
    )


def solution(mesh):
    rows_n, cols_n, reps = (mesh.shape[name] for name in ("row", "col", "rep"))
    if (rows_n, cols_n, reps) == (4, 4, 2):
        body = functools.partial(fused, rows_n, cols_n)
    else:
        body = gathered_form
    placed = (P("row", ("rep", "col")), P(("rep", "row"), "col"), P(), P(), P(), P())
    return jax.shard_map(
        body, mesh=mesh, in_specs=placed, out_specs=P("row", ("col", "rep")), check_vma=False
    )
```

```python
import functools

import jax
import jax.numpy as jnp
from jax import lax
from jax.experimental import pallas as pl
from jax.experimental.pallas import tpu as pltpu
from jax.sharding import PartitionSpec as P

TS = 128
PARTS = 4
SPLIT = 5


def remote(src, dst, send_sem, recv_sem, **target):
    return pltpu.make_async_remote_copy(
        src_ref=src,
        dst_ref=dst,
        send_sem=send_sem,
        recv_sem=recv_sem,
        device_id=target,
        device_id_type=pl.DeviceIdType.MESH,
    )


def kernel(
    a_ref,
    b_ref,
    mask_ref,
    k_ref,
    n_ref,
    stored_ref,
    out_ref,
    a_0,
    a_1,
    a_2,
    a_3,
    a_4,
    a_ord,
    a_far,
    b_all,
    part_out,
    part_in,
    fp_out,
    f_in,
    f_out,
    acc,
    own_sem,
    a_send,
    a_recv,
    b_send,
    b_recv,
    far_send,
    far_recv,
    fp_send,
    fp_recv,
    f_send,
    f_recv,
    p_send,
    p_recv,
):
    a_all = (a_0, a_1, a_2, a_3, a_4)
    z = lax.axis_index("row")
    c = lax.axis_index("col")
    r = lax.axis_index("rep")
    rows_n = b_all.shape[0]
    end = jnp.logical_or(z == 0, z == rows_n - 1)
    inner = jnp.logical_not(end)
    near = 2 * (z // 2)
    far = 2 - near
    buddy = z + 1 - 2 * (z % 2)
    across = rows_n - 1 - z
    beyond = rows_n - 1 - buddy
    x = c % 2
    y = c // 2
    xn = y * 2 + (1 - x)
    yn = (1 - y) * 2 + x
    diag = (1 - y) * 2 + (1 - x)
    mrow, kcol = a_ref.shape
    kb, ncol = b_ref.shape
    half = ncol // 2
    slots = kb // TS
    slab_tiles = slots * rows_n
    per = kcol // TS
    ra = mrow // PARTS
    steps = half // TS
    wide = half // 2
    mesh_id = pl.DeviceIdType.MESH

    def size(i):
        return ra if i < PARTS - 1 else ra // 2

    def start(i):
        return i * ra if i < PARTS else i * ra - ra // 2

    def rows(i):
        return pl.ds(start(i), size(i))

    own = [
        pltpu.make_async_copy(
            a_ref.at[rows(i), pl.ds(t * TS, TS)],
            a_all[i].at[c * per + t],
            own_sem.at[i, t],
        )
        for i in range(SPLIT)
        for t in range(per)
    ]
    for copy in own:
        copy.start()

    barrier = pltpu.get_barrier_semaphore()
    pl.semaphore_signal(barrier, inc=1, device_id={"col": xn}, device_id_type=mesh_id)
    pl.semaphore_signal(barrier, inc=1, device_id={"col": yn}, device_id_type=mesh_id)
    pl.semaphore_signal(barrier, inc=1, device_id={"rep": 1 - r}, device_id_type=mesh_id)
    pl.semaphore_signal(barrier, inc=1, device_id={"row": buddy}, device_id_type=mesh_id)

    @pl.when(inner)
    def _():
        pl.semaphore_signal(barrier, inc=1, device_id={"row": across}, device_id_type=mesh_id)

    def a_copy(kind, i, receive=False):
        link = kind % 2
        if kind < 2:
            owner = (xn, yn)[link] if receive else c
            view = a_all[i].at[pl.ds(owner * per, per)]
        else:
            owner = diag if receive else (yn, xn)[link]
            part = pl.ds(link * (size(i) // 2), size(i) // 2)
            view = a_all[i].at[pl.ds(owner * per, per), part, :]
        return remote(view, view, a_send.at[kind, i], a_recv.at[kind, i], col=(xn, yn)[link])

    def a_own(i):
        if i < SPLIT:
            a_copy(0, i).start()
            a_copy(1, i).start()

    def a_pass(i):
        a_copy(0, i, True).wait_recv()
        a_copy(3, i).start()
        a_copy(1, i, True).wait_recv()
        a_copy(2, i).start()

    def a_done(i):
        a_copy(2, i, True).wait_recv()
        a_copy(3, i, True).wait_recv()

    def tile_of(j):
        p = j // 2
        return ((1 - r) if j % 2 == 0 else r) * steps + p

    def lanes(t):
        return pl.ds(pl.multiple_of(t * TS, TS), TS)

    def b_copy(kind, j, receive=False):
        if receive:
            owner = (buddy, across, beyond, beyond, across)[kind]
        else:
            owner = (z, z, buddy, across, beyond)[kind]
        view = b_all.at[owner, :, lanes(tile_of(j))]
        target = across if kind in (1, 2) else buddy
        return remote(view, view, b_send.at[kind, j], b_recv.at[kind, j], row=target)

    def far_copy(kind, i, h, receive=False):
        side = (x, y)[h]
        at = pl.ds(start(i) + h * (size(i) // 2), size(i) // 2)
        if kind == 0:
            src = a_far.at[side, at, :] if receive else a_ord.at[far + side, at, :]
            dst = a_far.at[side, at, :]
            return remote(src, dst, far_send.at[0, i, h], far_recv.at[0, i, h], row=buddy)
        view = a_far.at[(1 - side) if receive else side, at, :]
        return remote(
            view, view, far_send.at[1, i, h], far_recv.at[1, i, h], col=(xn, yn)[h]
        )

    def piece(ref, i, p):
        return ref.at[i, p, pl.ds(0, size(i))]

    def fp_copy(i, p):
        return remote(
            piece(fp_out, i, p), piece(f_in, i, p), fp_send.at[i, p], fp_recv.at[i, p], rep=1 - r
        )

    def f_copy(i, p):
        return remote(
            piece(f_out, i, p), piece(f_in, i, p), f_send.at[i, p], f_recv.at[i, p], row=buddy
        )

    def swap(h):
        return remote(part_out.at[h], part_in.at[h], p_send.at[h], p_recv.at[h], rep=1 - r)

    def order(block, i):
        def one(s, carry):
            t = jnp.maximum(stored_ref[r * slab_tiles + block * slots + s] - r * slab_tiles, 0)
            a_ord[block, rows(i), lanes(s)] = a_all[i][t]
            return carry

        lax.fori_loop(0, slots, one, 0)

    def mask(j):
        tile = tile_of(j)
        g = c * (ncol // TS) + tile

        def one(t, carry):
            k = stored_ref[r * slab_tiles + z * slots + t]
            ok = jnp.logical_and(k_ref[k] == n_ref[g], mask_ref[g, k] == 1)
            weight = jnp.where(ok, 1.0, 0.0).astype(jnp.float32)
            at = pl.ds(pl.multiple_of(t * TS, TS), TS)
            value = b_ref[at, lanes(tile)].astype(jnp.float32) * weight
            b_all[z, at, lanes(tile)] = value.astype(jnp.bfloat16)
            return carry

        lax.fori_loop(0, slots, one, 0)

    def product(first, count, side, h):
        cols = pl.ds(pl.multiple_of(side * half + h * wide, wide), wide)

        def one(i):
            at = pl.ds(pl.multiple_of(i * ra, ra), ra)
            total = jnp.zeros((ra, wide), jnp.float32)
            for s in range(count):
                total += jnp.dot(
                    a_ord[first + s, at, :],
                    b_all[first + s, :, cols],
                    preferred_element_type=jnp.float32,
                )
            return at, total

        return one

    def send_partial(first, count, h):
        part = product(first, count, 1 - r, h)

        def away(i, carry):
            at, total = part(i)
            part_out[h, at, :] = total
            return carry

        lax.fori_loop(0, PARTS, away, 0)
        swap(h).start()

    def far_dot(i, j):
        total = jnp.zeros((size(i), TS), jnp.float32)
        for s in range(2):
            total += jnp.dot(
                a_far[s, rows(i), :],
                b_all[far + s, :, lanes(tile_of(j))],
                preferred_element_type=jnp.float32,
            )
        return total

    def far_away(pairs):
        for i, p in pairs:
            piece(fp_out, i, p)[...] = far_dot(i, 2 * p)
            fp_copy(i, p).start()

    def far_back(pairs):
        for i, p in pairs:
            total = far_dot(i, 2 * p + 1)
            fp_copy(i, p).wait_recv()
            piece(f_out, i, p)[...] = total + piece(f_in, i, p)[...]
            f_copy(i, p).start()

    chunks = 2 * steps
    for j in range(PARTS):
        mask(j)
    pl.semaphore_wait(barrier, 4 + jnp.where(inner, 1, 0))
    for j in range(PARTS):
        b_copy(0, j).start()
    for copy in own:
        copy.wait()
    a_own(0)
    a_own(1)
    for j in range(PARTS, chunks):
        mask(j)

    @pl.when(end)
    def _():
        sent = PARTS + 2
        b_copy(0, PARTS).start()
        b_copy(0, PARTS + 1).start()
        for i in range(SPLIT):
            a_pass(i)
            a_own(i + 2)
            a_done(i)
            order(far, i)
            order(far + 1, i)
            for h in range(2):
                far_copy(0, i, h).start()
            upto = min(chunks, sent + 2)
            for j in range(sent, upto):
                b_copy(0, j).start()
            sent = upto
        for i in range(SPLIT):
            order(near, i)
            order(near + 1, i)
        for j in range(chunks):
            b_copy(0, j, True).wait_recv()
        for h in (1, 0):
            if h == 0:
                for j in range(PARTS):
                    b_copy(3, j, True).wait_recv()
                    b_copy(4, j, True).wait_recv()
            first, count = (0, rows_n) if h == 0 else (near, 2)
            send_partial(first, count, h)
            part = product(first, count, r, h)

            def stay(i, carry, part=part, h=h):
                at, total = part(i)
                acc[at, pl.ds(h * wide, wide)] = total
                return carry

            lax.fori_loop(0, PARTS, stay, 0)
        swap(1).wait_recv()
        swap(0).wait_recv()

        def place(i, p, extra):
            value = acc[rows(i), pl.ds(p * TS, TS)]
            value = value + part_in[p // 2, rows(i), pl.ds((p % 2) * TS, TS)]
            if extra:
                value = value + piece(f_in, i, p)[...]
            out_ref[rows(i), pl.ds(p * TS, TS)] = value.astype(jnp.bfloat16)

        for i in range(SPLIT):
            place(i, 0, False)
            place(i, 1, False)
        for i, p in FAR_ORDER:
            f_copy(i, p).wait_recv()
            place(i, p, True)
        for i in range(SPLIT):
            for h in range(2):
                far_copy(0, i, h).wait_send()

    @pl.when(inner)
    def _():
        def pass_b(j):
            b_copy(1, j).start()
            b_copy(0, j, True).wait_recv()
            b_copy(2, j).start()

        def far_pass(i):
            for h in range(2):
                far_copy(0, i, h, True).wait_recv()
                far_copy(1, i, h).start()

        def raw(p):
            for j in (2 * p, 2 * p + 1):
                b_copy(3, j).start()
                b_copy(4, j).start()

        def far_got(i):
            for h in range(2):
                far_copy(1, i, h, True).wait_recv()

        def far_b(p):
            for j in (2 * p, 2 * p + 1):
                b_copy(1, j, True).wait_recv()
                b_copy(2, j, True).wait_recv()

        for j in range(PARTS, chunks):
            b_copy(0, j).start()
        pass_b(0)
        pass_b(1)
        a_pass(0)
        a_own(2)
        pass_b(2)
        pass_b(3)
        a_pass(1)
        a_own(3)
        pass_b(4)
        far_b(0)
        raw(0)
        pass_b(5)
        a_pass(2)
        a_own(4)
        far_b(1)
        raw(1)
        far_pass(0)
        a_pass(3)
        pass_b(6)
        pass_b(7)
        a_pass(4)
        for i in range(SPLIT):
            a_done(i)
            for s in range(rows_n):
                order(s, i)
        far_pass(1)
        send_partial(0, rows_n, 0)
        part = product(0, rows_n, r, 0)

        def keep(i, carry):
            at, total = part(i)
            acc[at, pl.ds(0, wide)] = total
            return carry

        lax.fori_loop(0, PARTS, keep, 0)
        far_b(2)
        far_got(0)
        far_got(1)
        far_away(FAR_ORDER[0:2])
        far_back(FAR_ORDER[0:2])
        far_pass(2)
        far_pass(3)
        far_got(2)
        far_away(FAR_ORDER[2:3])
        far_back(FAR_ORDER[2:3])
        far_pass(4)
        far_b(3)
        far_away(FAR_ORDER[3:6])
        far_got(3)
        far_away(FAR_ORDER[6:8])
        far_back(FAR_ORDER[3:6])
        far_got(4)
        far_away(FAR_ORDER[8:10])
        far_back(FAR_ORDER[6:10])
        send_partial(0, rows_n, 1)
        swap(0).wait_recv()
        out_ref[:, :wide] = (acc[:, :wide] + part_in[0]).astype(jnp.bfloat16)
        swap(1).wait_recv()
        part1 = product(0, rows_n, r, 1)

        def stay(i, carry):
            at, total = part1(i)
            out_ref[at, pl.ds(wide, wide)] = (total + part_in[1, at, :]).astype(jnp.bfloat16)
            return carry

        lax.fori_loop(0, PARTS, stay, 0)
        for i, p in FAR_ORDER:
            fp_copy(i, p).wait_send()
            f_copy(i, p).wait_send()
        for i in range(SPLIT):
            for h in range(2):
                far_copy(1, i, h).wait_send()
        for j in range(chunks):
            b_copy(1, j).wait_send()
            b_copy(2, j).wait_send()
        for j in range(PARTS):
            b_copy(3, j).wait_send()
            b_copy(4, j).wait_send()

    for h in range(2):
        swap(h).wait_send()
    for i in range(SPLIT):
        for kind in range(4):
            a_copy(kind, i).wait_send()
    for j in range(chunks):
        b_copy(0, j).wait_send()


FAR_ORDER = (
    (0, 2), (1, 2), (2, 2),
    (0, 3), (1, 3), (2, 3),
    (3, 2), (3, 3), (4, 2), (4, 3),
)


def fused(rows_n, cols_n, amplitudes, integrals, tile_mask, k_irrep, n_irrep, stored_tile):
    mrow, kcol = amplitudes.shape
    kb, ncol = integrals.shape
    half = ncol // 2
    steps = half // TS
    smem = pl.BlockSpec(memory_space=pltpu.SMEM)
    vmem = pl.BlockSpec(memory_space=pltpu.VMEM)
    tiles = pltpu.VMEM((SPLIT, steps, mrow // PARTS, TS), jnp.float32)
    chunk = pltpu.VMEM((cols_n * kcol // TS, mrow // PARTS, TS), jnp.bfloat16)
    last = pltpu.VMEM((cols_n * kcol // TS, mrow // PARTS // 2, TS), jnp.bfloat16)
    dma = pltpu.SemaphoreType.DMA
    return pl.pallas_call(
        kernel,
        out_shape=jax.ShapeDtypeStruct((mrow, half), jnp.bfloat16),
        in_specs=[pl.BlockSpec(memory_space=pl.ANY), vmem, smem, smem, smem, smem],
        out_specs=vmem,
        scratch_shapes=[
            chunk,
            chunk,
            chunk,
            last,
            last,
            pltpu.VMEM((rows_n, mrow, kb), jnp.bfloat16),
            pltpu.VMEM((2, mrow, kb), jnp.bfloat16),
            pltpu.VMEM((rows_n, kb, ncol), jnp.bfloat16),
            pltpu.VMEM((2, mrow, half // 2), jnp.float32),
            pltpu.VMEM((2, mrow, half // 2), jnp.float32),
            tiles,
            tiles,
            tiles,
            pltpu.VMEM((mrow, half), jnp.float32),
            dma((SPLIT, kcol // TS)),
            dma((4, SPLIT)),
            dma((4, SPLIT)),
            dma((5, 2 * steps)),
            dma((5, 2 * steps)),
            dma((2, SPLIT, 2)),
            dma((2, SPLIT, 2)),
            dma((SPLIT, steps)),
            dma((SPLIT, steps)),
            dma((SPLIT, steps)),
            dma((SPLIT, steps)),
            dma((2,)),
            dma((2,)),
        ],
        compiler_params=pltpu.CompilerParams(
            collective_id=0, has_side_effects=True, vmem_limit_bytes=56 << 20
        ),
        cost_estimate=pl.CostEstimate(
            flops=2 * mrow * kb * rows_n * ncol,
            bytes_accessed=2 * (mrow * kcol + kb * ncol + mrow * half),
            transcendentals=0,
        ),
    )(amplitudes, integrals, tile_mask.T, k_irrep, n_irrep, stored_tile)


def gathered_form(amplitudes, integrals, tile_mask, k_irrep, n_irrep, stored_tile):
    slab = lax.axis_index("rep")
    column = lax.axis_index("col")
    place = lax.axis_index("row")
    kb, ncol = integrals.shape
    tiles_col = ncol // TS
    own = kb // TS
    slab_tiles = own * lax.axis_size("row")
    n_labels = lax.dynamic_slice_in_dim(n_irrep, column * tiles_col, tiles_col)
    mask_cols = lax.dynamic_slice_in_dim(tile_mask, column * tiles_col, tiles_col, 1)
    slots = lax.dynamic_slice_in_dim(stored_tile, slab * slab_tiles, slab_tiles)
    mine = lax.dynamic_slice_in_dim(slots, place * own, own)
    same = jnp.take(k_irrep, mine)[:, None] == n_labels[None, :]
    weights = jnp.logical_and(same, jnp.take(mask_cols, mine, axis=0) == 1).astype(jnp.bfloat16)
    shaped = integrals.reshape(own, TS, tiles_col, TS) * weights[:, None, :, None]
    masked = lax.all_gather(shaped.reshape(kb, ncol), "row", axis=0, tiled=True)
    amp_slab = lax.all_gather(amplitudes, "col", axis=1, tiled=True)
    mrow, kq = amp_slab.shape
    ordered = jnp.take(
        amp_slab.reshape(mrow, slab_tiles, TS), slots - slab * slab_tiles, axis=1
    ).reshape(mrow, kq)
    partial_value = jnp.dot(ordered, masked, preferred_element_type=jnp.float32)
    return lax.psum_scatter(partial_value, "rep", scatter_dimension=1, tiled=True).astype(
        jnp.bfloat16
    )


def solution(mesh):
    rows_n, cols_n, reps = (mesh.shape[name] for name in ("row", "col", "rep"))
    if (rows_n, cols_n, reps) == (4, 4, 2):
        body = functools.partial(fused, rows_n, cols_n)
    else:
        body = gathered_form
    placed = (P("row", ("rep", "col")), P(("rep", "row"), "col"), P(), P(), P(), P())
    return jax.shard_map(
        body, mesh=mesh, in_specs=placed, out_specs=P("row", ("col", "rep")), check_vma=False
    )
```
